32 devices in a mesh: lat: 4 (over y, x), lon: 8 (over z, core).
Axes of the slice: x: 2, y: 2, z: 4, core: 2. Of those that a mesh axis runs over, the one named last changes fastest.
Arguments:
- fields: bfloat16 [448, 896, 768], P('lat', 'lon'), may hold values from -6 to 6
- cotangent: bfloat16 [448, 896, 768], P('lat', 'lon'), may hold values from -6 to 6
- inner_weight: bfloat16 [8, 2, 96, 96], replicated, may hold values from -0.4375 to 0.4375
- outer_weight: bfloat16 [8, 2, 96, 96], replicated, may hold values from -0.4375 to 0.4375
Outputs:
- field_gradient: bfloat16 [448, 896, 768], P('lat', 'lon')
- inner_gradient: float32 [8, 2, 96, 96], replicated
- outer_gradient: float32 [8, 2, 96, 96], replicated
The draws below stay inside these ranges and needn't reach their ends.
All inputs are finite; a program needn't handle non-finite values.
Results may differ from the reference program's by a relative error of at most 0.012.
Values may be sent and summed in bfloat16 or wider, within the bound.
No kernel may reach another device: no remote copies, remote signals or barrier semaphores. Data moves between devices by JAX's collectives and lax.ppermute only.
A program may use at most 256 MiB of HBM per device.

```python
import math
import jax
import jax.numpy as jnp

LATS = 448
LONS = 896
MODES = 128
WIDTH = 768
BLOCKS = 8
BLOCK_W = 96


def block_levels(own_key, extent, cuts, low, top_value):
    level, own = 1.0, jax.random.fold_in(own_key, 6)
    for axis_at, parts in cuts:
        draws = jnp.exp(jax.random.uniform(jax.random.fold_in(own, axis_at), (parts,), jnp.float32, low / len(cuts), top_value / len(cuts)))
        level = level * jnp.repeat(draws, extent[axis_at] // parts).reshape([-1 if axis == axis_at else 1 for axis in range(len(extent))])
    return level


def centred(key, extent, deviation, reach, split=(), kind=jnp.bfloat16):
    drawn = deviation * jax.random.normal(key, extent, jnp.float32)
    if split:
        drawn = drawn * block_levels(key, extent, split, -0.22, 0.18)
    return jnp.clip(drawn, -reach, reach).astype(kind)


def setup_inputs(seed: int = 0) -> dict:
    seeds = jax.random.split(jax.random.key(seed), 5)
    fields = centred(seeds[0], (LATS, LONS, WIDTH), 1.0, 6.0, ((0, 4), (1, 8)))
    cotangent = centred(seeds[1], (LATS, LONS, WIDTH), 1.0, 6.0, ((0, 4), (1, 8)))
    inner_weight = centred(seeds[2], (BLOCKS, 2, BLOCK_W, BLOCK_W), (2 * BLOCK_W) ** -0.5, 0.4375)
    outer_weight = centred(seeds[3], (BLOCKS, 2, BLOCK_W, BLOCK_W), (2 * BLOCK_W) ** -0.5, 0.4375)
    return dict(fields=fields, cotangent=cotangent, inner_weight=inner_weight, outer_weight=outer_weight)


def tables(row_total, col_total, period, row_first, col_first):
    row_ids = row_first + jnp.arange(row_total, dtype=jnp.int32)
    col_ids = col_first + jnp.arange(col_total, dtype=jnp.int32)
    phase = (row_ids[:, None] * col_ids[None, :] % period).astype(jnp.float32) * (2.0 * math.pi / period)
    factor = 1.0 / math.sqrt(period)
    return ((jnp.cos(phase) * factor).astype(jnp.bfloat16), (jnp.sin(phase) * factor).astype(jnp.bfloat16))

def gelu_pair(value):
    cdf = 0.5 * (1.0 + jax.scipy.special.erf(value * 0.7071067811865476))
    density = jnp.exp(-0.5 * value * value) * 0.3989422804014327
    return (value * cdf, cdf + value * density)

def widen(value):
    return value.astype(jnp.float32)

def complex_apply(left_r, left_i, weight):
    real_w = widen(weight[:, 0])
    imag_w = widen(weight[:, 1])
    real = jnp.einsum('pbi,bij->pbj', widen(left_r), real_w) - jnp.einsum('pbi,bij->pbj', widen(left_i), imag_w)
    imag = jnp.einsum('pbi,bij->pbj', widen(left_r), imag_w) + jnp.einsum('pbi,bij->pbj', widen(left_i), real_w)
    return (real, imag)

def complex_adjoint(adj_r, adj_i, weight):
    real_w = widen(weight[:, 0])
    imag_w = widen(weight[:, 1])
    real = jnp.einsum('pbj,bij->pbi', widen(adj_r), real_w) + jnp.einsum('pbj,bij->pbi', widen(adj_i), imag_w)
    imag = jnp.einsum('pbj,bij->pbi', widen(adj_i), real_w) - jnp.einsum('pbj,bij->pbi', widen(adj_r), imag_w)
    return (real, imag)

def complex_outer(left_r, left_i, adj_r, adj_i):
    real = jnp.einsum('pbi,pbj->bij', widen(left_r), widen(adj_r)) + jnp.einsum('pbi,pbj->bij', widen(left_i), widen(adj_i))
    imag = jnp.einsum('pbi,pbj->bij', widen(left_r), widen(adj_i)) - jnp.einsum('pbi,pbj->bij', widen(left_i), widen(adj_r))
    return jnp.stack([real, imag], axis=1)

def lat_forward(lat_cos, lat_sin, part_r, part_i):
    flat_r = part_r.reshape(LATS, -1)
    flat_i = part_i.reshape(LATS, -1)
    real = jnp.dot(lat_cos, flat_r, preferred_element_type=jnp.float32) + jnp.dot(lat_sin, flat_i, preferred_element_type=jnp.float32)
    imag = jnp.dot(lat_cos, flat_i, preferred_element_type=jnp.float32) - jnp.dot(lat_sin, flat_r, preferred_element_type=jnp.float32)
    return (real.astype(jnp.bfloat16).reshape(-1, BLOCKS, BLOCK_W), imag.astype(jnp.bfloat16).reshape(-1, BLOCKS, BLOCK_W))

def reference(fields, cotangent, inner_weight, outer_weight):
    lon_cos, lon_sin = tables(MODES, LONS, LONS, 0, 0)
    factor = jnp.where(jnp.arange(MODES) == 0, 1.0, 2.0).astype(jnp.bfloat16)[:, None]
    forward_table = jnp.concatenate([lon_cos, -lon_sin], axis=0)
    pull_table = jnp.concatenate([lon_cos * factor, -(lon_sin * factor)], axis=0)
    spectrum = jnp.einsum('kw,hwc->hkc', widen(forward_table), widen(fields)).astype(jnp.bfloat16)
    pulled = jnp.einsum('kw,hwc->hkc', widen(pull_table), widen(cotangent)).astype(jnp.bfloat16)
    lat_cos, lat_sin = tables(LATS, LATS, LATS, 0, 0)
    z_r, z_i = lat_forward(lat_cos, lat_sin, spectrum[:, :MODES], spectrum[:, MODES:])
    back_r, back_i = lat_forward(lat_cos, lat_sin, pulled[:, :MODES], pulled[:, MODES:])
    u_r, u_i = complex_apply(z_r, z_i, inner_weight)
    gelu_r, slope_r = gelu_pair(u_r)
    gelu_i, slope_i = gelu_pair(u_i)
    hidden_r = gelu_r.astype(jnp.bfloat16)
    hidden_i = gelu_i.astype(jnp.bfloat16)
    hidden_adj_r, hidden_adj_i = complex_adjoint(back_r, back_i, outer_weight)
    u_adj_r = (hidden_adj_r * slope_r).astype(jnp.bfloat16)
    u_adj_i = (hidden_adj_i * slope_i).astype(jnp.bfloat16)
    scale = 1.0 / math.sqrt(LATS * MODES)
    outer_gradient = complex_outer(hidden_r, hidden_i, back_r, back_i) * scale
    inner_gradient = complex_outer(z_r, z_i, u_adj_r, u_adj_i) * scale
    z_adj_r, z_adj_i = complex_adjoint(u_adj_r, u_adj_i, inner_weight)
    flat_r = z_adj_r.astype(jnp.bfloat16).reshape(LATS, -1)
    flat_i = z_adj_i.astype(jnp.bfloat16).reshape(LATS, -1)
    cos_back = lat_cos.T
    sin_back = lat_sin.T
    adj_r = jnp.dot(cos_back, flat_r, preferred_element_type=jnp.float32) - jnp.dot(sin_back, flat_i, preferred_element_type=jnp.float32)
    adj_i = jnp.dot(sin_back, flat_r, preferred_element_type=jnp.float32) + jnp.dot(cos_back, flat_i, preferred_element_type=jnp.float32)
    adj_r = adj_r.astype(jnp.bfloat16).reshape(LATS, MODES, WIDTH)
    adj_i = adj_i.astype(jnp.bfloat16).reshape(LATS, MODES, WIDTH)
    merged = jnp.concatenate([adj_r, adj_i], axis=1)
    field_gradient = jnp.einsum('hkc,kw->hwc', widen(merged), widen(forward_table)).astype(jnp.bfloat16)
    return (field_gradient, inner_gradient, outer_gradient)
```

```python
import functools
import math

import jax
import jax.numpy as jnp
from jax import lax
from jax.experimental import pallas as pl
from jax.experimental.pallas import tpu as pltpu
from jax.sharding import PartitionSpec as P

LATS = 448
LONS = 896
MODES = 128
BLOCKS = 8
BLOCK_W = 96
PARTS = 2
DELAY = 2
LANES = 128
VMEM = 58 * 1024 * 1024
F32 = jnp.float32
BF16 = jnp.bfloat16


def trig_rows(row_ids, col_ids, period):
    phase = (row_ids[:, None] * col_ids[None, :] % period).astype(F32) * (2.0 * math.pi / period)
    factor = 1.0 / math.sqrt(period)
    return (
        (jnp.cos(phase) * factor).astype(BF16),
        (jnp.sin(phase) * factor).astype(BF16),
    )


def gelu_pair(value):
    cdf = 0.5 * (1.0 + lax.erf(value * 0.7071067811865476))
    density = jnp.exp(-0.5 * value * value) * 0.3989422804014327
    return (value * cdf, cdf + value * density)


def dot(left, right, left_dim=1, right_dim=0):
    return lax.dot_general(
        left, right, (((left_dim,), (right_dim,)), ((), ())), preferred_element_type=F32
    )


def params():
    return pltpu.CompilerParams(vmem_limit_bytes=VMEM)


def hop_body(t, row_block, has_recv, has_prev, has_final, scal, *refs):
    refs = list(refs)
    up_in, down_in = refs[0:5], refs[5:10]
    at = 10
    recv_up = recv_down = None
    if has_recv:
        recv_up, recv_down = refs[at : at + 2]
        at += 2
    if has_prev:
        at += 1
    up_out, down_out = refs[at : at + 2]
    at += 2
    final = None
    if has_final:
        final = refs[at]
        at += 1
    up_sum, down_sum = refs[at : at + 2]
    step = pl.program_id(0)
    sub, _, half = up_in[0].shape
    coefs = up_out.shape[0]
    tiles = half // LANES
    for column, (fields, cot, fields_other, cot_other, table), total in (
        (0, up_in, up_sum),
        (3, down_in, down_sum),
    ):
        def work(mine, other, table=table, total=total):
            own_table = table[0, 0, 0, 0]
            other_table = table[0, 0, 0, 1]
            for h in range(sub):
                value = dot(own_table, mine[h]) + dot(other_table, other[h])
                for j in range(tiles):
                    total[j, pl.ds(step * sub + h, coefs, stride=row_block), :] = value[
                        :, j * LANES : (j + 1) * LANES
                    ]

        pl.when(scal[t, column] == 0)(functools.partial(work, fields, fields_other))
        pl.when(scal[t, column] != 0)(functools.partial(work, cot, cot_other))

    @pl.when(step == pl.num_programs(0) - 1)
    def _():
        for total, recv, out in ((up_sum, recv_up, up_out), (down_sum, recv_down, down_out)):
            for j in range(tiles):
                lanes = pl.ds(j * LANES, LANES)
                value = total[j].reshape(coefs, row_block, LANES)
                if has_recv:
                    value = value + recv[:, :, lanes].astype(F32)
                out[:, :, lanes] = value.astype(BF16)
        if has_final:
            @pl.when(scal[t, 7] == 0)
            def _():
                final[...] = down_out[...]

            @pl.when(scal[t, 7] != 0)
            def _():
                final[...] = up_out[...]


def hop(t, scal, arrays, tables, recv, prev, final_at, row_block, rows):
    fields, cot, fields_other, cot_other = arrays
    cols = fields.shape[1]
    half = fields_other.shape[2]
    coefs = tables.shape[4]
    sub = 4
    steps = row_block // sub
    has_final = final_at is not None
    once = pl.Buffered(1)

    def mine(column):
        return pl.BlockSpec(
            (sub, cols, half), lambda i, s: (s[t, column + 1] * steps + i, 0, s[t, 6])
        )

    def other(column):
        return pl.BlockSpec((sub, cols, half), lambda i, s: (s[t, column + 1] * steps + i, 0, 0))

    def table(column, end):
        return pl.BlockSpec(
            (1, 1, 1, 2, coefs, cols),
            lambda i, s: (s[t, column + 2], s[t, column], end, 0, 0, 0),
            pipeline_mode=once,
        )

    piece = pl.BlockSpec((coefs, row_block, half), lambda i, s: (0, 0, 0), pipeline_mode=once)
    in_specs = []
    operands = []
    for column, end in ((0, 1), (3, 0)):
        in_specs += [mine(column), mine(column), other(column), other(column), table(column, end)]
        operands += [fields, cot, fields_other, cot_other, tables]
    if recv is not None:
        in_specs += [piece, piece]
        operands += list(recv)
    aliases = {}
    if prev is not None:
        in_specs.append(pl.BlockSpec(memory_space=pl.ANY))
        aliases[1 + len(operands)] = 2
        operands.append(prev)
    out_shape = [jax.ShapeDtypeStruct((coefs, row_block, half), BF16)] * 2
    out_specs = [piece, piece]
    if has_final:
        out_shape.append(jax.ShapeDtypeStruct((coefs, rows, half), BF16))
        out_specs.append(
            pl.BlockSpec((coefs, row_block, half), lambda i, s: (0, final_at, 0))
        )
    chunk = pltpu.VMEM((half // LANES, coefs * row_block, LANES), F32)
    return pl.pallas_call(
        functools.partial(
            hop_body, t, row_block, recv is not None, prev is not None, has_final
        ),
        grid_spec=pltpu.PrefetchScalarGridSpec(
            num_scalar_prefetch=1,
            grid=(steps,),
            in_specs=in_specs,
            out_specs=out_specs,
            scratch_shapes=[chunk, chunk],
        ),
        out_shape=out_shape,
        input_output_aliases=aliases,
        compiler_params=params(),
        cost_estimate=pl.CostEstimate(
            flops=8 * row_block * coefs * cols * half,
            bytes_accessed=16 * row_block * cols * half,
            transcendentals=0,
        ),
        name="longitude_hop",
    )(scal, *operands)


def filter_body(
    spectrum, pulled, forward, backward, inner, inner_t, outer_t,
    adjoint, inner_gradient, outer_gradient, stack, z, back, hidden, u_adj,
):
    bands, _, _, rows, half = spectrum.shape
    lats = bands * rows
    tile = lats // 4

    @pl.when(pl.program_id(0) == 0)
    def _():
        inner_gradient[...] = jnp.zeros_like(inner_gradient)
        outer_gradient[...] = jnp.zeros_like(outer_gradient)

    for source, target in ((spectrum, z), (pulled, back)):
        for part in range(2):
            for band in range(bands):
                first = part * lats + band * rows
                stack[first : first + rows, :] = source[band, part, 0]
        for part in range(2):
            @pl.loop(0, 2)
            def _(i, part=part, target=target):
                at = pl.multiple_of(i * 2 * tile, 16)
                value = dot(forward[pl.ds(part * lats + at, 2 * tile), :], stack[...])
                target[pl.ds(at, 2 * tile), part * half : (part + 1) * half] = value.astype(BF16)

    @pl.loop(0, 4)
    def _(i):
        at = pl.ds(pl.multiple_of(i * tile, 16), tile)
        gelu, slope = gelu_pair(dot(z[at, :], inner[...]))
        hidden[at, :] = gelu.astype(BF16)
        u_adj[at, :] = (dot(back[at, :], outer_t[...]) * slope).astype(BF16)
        z_adj = dot(u_adj[at, :], inner_t[...]).astype(BF16)
        for part in range(2):
            where = pl.ds(pl.multiple_of(part * lats + i * tile, 16), tile)
            stack[where, :] = z_adj[:, part * half : (part + 1) * half]

    outer_gradient[...] += dot(hidden[...], back[...], 0, 0)
    inner_gradient[...] += dot(z[...], u_adj[...], 0, 0)
    for part in range(2):
        for band in range(bands):
            first = part * lats + band * rows
            value = dot(backward[first : first + rows, :], stack[...])
            adjoint[band, part, 0] = value.astype(BF16)


def spectral_filter(spectrum, pulled, forward, backward, inner, inner_t, outer_t):
    bands, _, modes, rows, half = spectrum.shape
    lats = bands * rows
    wide = 2 * half
    data = pl.BlockSpec((bands, 2, 1, rows, half), lambda i: (0, 0, i, 0, 0))

    def whole(*shape):
        return pl.BlockSpec(shape, lambda i: (0,) * len(shape), pipeline_mode=pl.Buffered(1))

    square = whole(2 * lats, 2 * lats)
    weight = whole(wide, wide)
    return pl.pallas_call(
        filter_body,
        grid=(modes,),
        in_specs=[data, data, square, square, weight, weight, weight],
        out_specs=[data, weight, weight],
        out_shape=[
            jax.ShapeDtypeStruct(spectrum.shape, BF16),
            jax.ShapeDtypeStruct((wide, wide), F32),
            jax.ShapeDtypeStruct((wide, wide), F32),
        ],
        scratch_shapes=[
            pltpu.VMEM((2 * lats, half), BF16),
            pltpu.VMEM((lats, wide), BF16),
            pltpu.VMEM((lats, wide), BF16),
            pltpu.VMEM((lats, wide), BF16),
            pltpu.VMEM((lats, wide), BF16),
        ],
        compiler_params=params(),
        cost_estimate=pl.CostEstimate(
            flops=modes * 2 * (3 * 4 * lats * lats * half + 5 * lats * wide * wide),
            bytes_accessed=6 * modes * 2 * lats * half,
            transcendentals=modes * 2 * lats * half * 2,
        ),
        name="spectral_filter",
    )(spectrum, pulled, forward, backward, inner, inner_t, outer_t)


def relay_body(t, has_own, has_recv, has_prev, scal, *refs):
    refs = list(refs)
    own = refs.pop(0) if has_own else None
    recv = (refs.pop(0), refs.pop(0)) if has_recv else None
    if has_prev:
        refs = refs[2:]
    sends, kept = refs[0:2], refs[2:4]
    for way in range(2):
        def put(value, way=way):
            sends[way][...] = value[...]
            kept[way][0] = value[...]

        if own is None:
            put(recv[way])
        elif recv is None:
            put(own)
        else:
            pl.when(scal[t, 2 + way] != 0)(functools.partial(put, own))
            pl.when(scal[t, 2 + way] == 0)(functools.partial(put, recv[way]))


def relay(t, scal, own, own_at, recv, prev, count, shape):
    coefs, row_block, half = shape
    piece = pl.BlockSpec(shape, lambda i, s: (0, 0, 0))
    in_specs, operands = [], []
    if own is not None:
        in_specs.append(pl.BlockSpec(shape, lambda i, s: (0, own_at, 0)))
        operands.append(own)
    if recv is not None:
        in_specs += [piece, piece]
        operands += list(recv)
    aliases = {}
    if prev is not None:
        for i, array in enumerate(prev):
            aliases[1 + len(operands)] = 2 + i
            in_specs.append(pl.BlockSpec(memory_space=pl.ANY))
            operands.append(array)

    def kept(way):
        return pl.BlockSpec((1,) + shape, lambda i, s: (s[t, way], 0, 0, 0))

    return pl.pallas_call(
        functools.partial(relay_body, t, own is not None, recv is not None, prev is not None),
        grid_spec=pltpu.PrefetchScalarGridSpec(
            num_scalar_prefetch=1,
            grid=(1,),
            in_specs=in_specs,
            out_specs=[piece, piece, kept(0), kept(1)],
        ),
        out_shape=[jax.ShapeDtypeStruct(shape, BF16)] * 2
        + [jax.ShapeDtypeStruct((count + 1,) + shape, BF16)] * 2,
        input_output_aliases=aliases,
        compiler_params=params(),
        cost_estimate=pl.CostEstimate(
            flops=0, bytes_accessed=8 * coefs * row_block * half, transcendentals=0
        ),
        name="relay",
    )(scal, *operands)


def grid_body(core, *refs):
    pieces, panels, (own_out, other_out, *totals) = (
        refs[: 2 * PARTS], refs[2 * PARTS], refs[2 * PARTS + 1 :]
    )
    _, coefs, row_block, half = pieces[0].shape
    tiles = half // LANES
    for total, piece in zip(totals, pieces):
        for j in range(tiles):
            value = piece[0, :, :, pl.ds(j * LANES, LANES)].astype(F32)
            total[j] = value.reshape(coefs * row_block, LANES)
    for h in range(row_block):
        rows = [
            jnp.concatenate(
                [total[j, pl.ds(h, coefs, stride=row_block), :] for j in range(tiles)], axis=1
            ).astype(BF16)
            for total in totals
        ]
        value = jnp.concatenate(rows, axis=0)
        own_out[h] = dot(panels[0], value).astype(BF16)
        other_out[h] = dot(panels[1], value).astype(BF16)


def to_grid(core, kept, panels, rows, width):
    _, coefs, row_block, half = kept[0].shape
    blocks = rows // row_block
    cols = panels.shape[1]

    def piece(part):
        return pl.BlockSpec(
            (1, coefs, row_block, half), lambda i, s: (part * blocks + i, 0, 0, 0)
        )

    total = pltpu.VMEM((half // LANES, coefs * row_block, LANES), F32)
    return pl.pallas_call(
        grid_body,
        grid_spec=pltpu.PrefetchScalarGridSpec(
            num_scalar_prefetch=1,
            grid=(blocks,),
            in_specs=[piece(part) for _ in range(2) for part in range(PARTS)]
            + [pl.BlockSpec(panels.shape, lambda i, s: (0, 0, 0))],
            out_specs=[
                pl.BlockSpec((row_block, cols, half), lambda i, s: (i, 0, s[0])),
                pl.BlockSpec((row_block, cols, half), lambda i, s: (i, 0, 0)),
            ],
            scratch_shapes=[total] * (2 * PARTS),
        ),
        out_shape=[
            jax.ShapeDtypeStruct((rows, cols, width), BF16),
            jax.ShapeDtypeStruct((rows, cols, half), BF16),
        ],
        compiler_params=params(),
        cost_estimate=pl.CostEstimate(
            flops=8 * PARTS * rows * coefs * cols * half,
            bytes_accessed=4 * (PARTS * coefs + cols) * rows * half,
            transcendentals=0,
        ),
        name="longitude_grid",
    )(core, *[array for array in kept for _ in range(PARTS)], panels)


def place_body(core, piece, whole, out):
    out[...] = piece[...]


def place(core, piece, whole, row_block):
    rows, cols, half = piece.shape
    return pl.pallas_call(
        place_body,
        grid_spec=pltpu.PrefetchScalarGridSpec(
            num_scalar_prefetch=1,
            grid=(rows // row_block,),
            in_specs=[
                pl.BlockSpec((row_block, cols, half), lambda i, s: (i, 0, 0)),
                pl.BlockSpec(memory_space=pl.ANY),
            ],
            out_specs=pl.BlockSpec((row_block, cols, half), lambda i, s: (i, 0, 1 - s[0])),
        ),
        out_shape=jax.ShapeDtypeStruct(whole.shape, BF16),
        input_output_aliases={2: 0},
        compiler_params=params(),
        name="place",
    )(core, piece, whole)


def block_diagonal(blocks):
    count, size, _ = blocks.shape
    eye = jnp.eye(count, dtype=blocks.dtype)
    wide = blocks[:, :, None, :] * eye[:, None, :, None]
    return wide.reshape(count * size, count * size)


def complex_weight(weight):
    real = block_diagonal(weight[:, 0])
    imag = block_diagonal(weight[:, 1])
    return jnp.concatenate(
        [
            jnp.concatenate([real, imag], axis=1),
            jnp.concatenate([-imag, real], axis=1),
        ],
        axis=0,
    )


def gradient_blocks(total, half):
    real = total[:half, :half] + total[half:, half:]
    imag = total[:half, half:] - total[half:, :half]
    parts = []
    for b in range(half // BLOCK_W):
        at = slice(b * BLOCK_W, (b + 1) * BLOCK_W)
        parts.append(jnp.stack([real[at, at], imag[at, at]], axis=0))
    return jnp.stack(parts, axis=0)


def local(fields, cotangent, inner_weight, outer_weight):
    lat_count = lax.axis_size("lat")
    lon_count = lax.axis_size("lon")
    rows, cols, width = fields.shape
    chips = lon_count // 2
    half = width // 2
    lon = lax.axis_index("lon")
    chip = lon // 2
    core = lon % 2
    row_block = 16 if rows % 16 == 0 else 8
    blocks = rows // row_block
    per_end = MODES // 2
    per_group = per_end // lat_count
    per_part = per_group // PARTS
    coefs = lat_count * 2 * per_part
    swap = [(i, i ^ 1) for i in range(lon_count)]
    upward = [(i, i + 2) for i in range(lon_count - 2)]
    downward = [(i + 2, i) for i in range(lon_count - 2)]

    def other_half(array):
        return lax.dynamic_slice_in_dim(array, (1 - core) * half, half, axis=2)

    fields_other = lax.ppermute(other_half(fields), "lon", swap)
    cot_other = lax.ppermute(other_half(cotangent), "lon", swap)

    q = jnp.arange(coefs, dtype=jnp.int32)
    part_of = q // per_part % 2
    ids = q // (2 * per_part) * per_group + q % per_part
    ends = jnp.arange(2, dtype=jnp.int32)[:, None, None] * per_end
    pieces = jnp.arange(PARTS, dtype=jnp.int32)[None, :, None] * per_part
    mode_ids = (ends + pieces + ids).reshape(-1)
    imag_row = jnp.tile(part_of, 2 * PARTS) == 1
    places = jnp.concatenate(
        [lon * cols + jnp.arange(cols, dtype=jnp.int32),
         (lon ^ 1) * cols + jnp.arange(cols, dtype=jnp.int32)]
    )
    cos_rows, sin_rows = trig_rows(mode_ids, places, LONS)
    base = jnp.where(imag_row[:, None], -sin_rows, cos_rows)
    weights = jnp.where(mode_ids == 0, 1.0, 2.0).astype(BF16)
    both = jnp.stack([base, base * weights[:, None]], axis=0)
    tables = both.reshape(2, 2, PARTS, coefs, 2, cols).transpose(2, 0, 1, 4, 3, 5)
    panels = base.T.reshape(2, cols, 2 * PARTS * coefs)

    lat_ids = jnp.arange(LATS, dtype=jnp.int32)
    lat_cos, lat_sin = trig_rows(lat_ids, lat_ids, LATS)
    forward = jnp.concatenate(
        [jnp.concatenate([lat_cos, lat_sin], axis=1),
         jnp.concatenate([-lat_sin, lat_cos], axis=1)], axis=0
    )
    backward = jnp.concatenate(
        [jnp.concatenate([lat_cos, -lat_sin], axis=1),
         jnp.concatenate([lat_sin, lat_cos], axis=1)], axis=0
    )
    own_blocks = half // BLOCK_W
    inner = complex_weight(
        lax.dynamic_slice_in_dim(inner_weight, core * own_blocks, own_blocks, axis=0)
    )
    outer = complex_weight(
        lax.dynamic_slice_in_dim(outer_weight, core * own_blocks, own_blocks, axis=0)
    )
    inner_t, outer_t = inner.T, outer.T

    order = [(s, a, r) for s in range(PARTS) for a in range(2) for r in range(blocks)]
    count = len(order)
    slots = count + DELAY * (chips - 1)
    slot_ids = jnp.arange(slots, dtype=jnp.int32)

    def schedule(late):
        v = jnp.clip(slot_ids - DELAY * late, 0, count - 1)
        return [v // blocks % 2, v % blocks, v // (2 * blocks)]

    flat = jnp.zeros_like(slot_ids)
    scal = jnp.stack(
        schedule(chip) + schedule(chips - 1 - chip) + [flat + core, flat + chip], axis=1
    )
    sent = {}
    gathered = {}
    for t in range(slots):
        v = t - DELAY * (chips - 1)
        early = t < blocks
        arrays = (
            fields,
            fields if early else cotangent,
            fields_other,
            fields_other if early else cot_other,
        )
        recv = sent.pop(t - DELAY, None)
        key, final_at, prev = None, None, None
        if v >= 0:
            key, final_at = order[v][:2], order[v][2]
            prev = gathered.get(key)
        result = hop(t, scal, arrays, tables, recv, prev, final_at, row_block, rows)
        if v >= 0:
            gathered[key] = result[2]
        if t < count + DELAY * (chips - 2):
            sent[t] = (
                lax.ppermute(result[0], "lon", upward),
                lax.ppermute(result[1], "lon", downward),
            )

    def across(array):
        return lax.all_to_all(array, "lat", split_axis=0, concat_axis=0, tiled=True)

    spread = []
    inner_total = outer_total = 0.0
    for s in range(PARTS):
        shape = (lat_count, 2, per_part, rows, half)
        adjoint, inner_part, outer_part = spectral_filter(
            across(gathered[s, 0]).reshape(shape),
            across(gathered[s, 1]).reshape(shape),
            forward, backward, inner, inner_t, outer_t,
        )
        inner_total = inner_total + inner_part
        outer_total = outer_total + outer_part
        spread.append(across(adjoint.reshape(coefs, rows, half)))
    at_end = (chip == 0) | (chip == chips - 1)
    sums = jnp.stack([gradient_blocks(inner_total, half), gradient_blocks(outer_total, half)])
    sums = jnp.where(at_end, sums, 0.0)
    empty = jnp.zeros((2, BLOCKS) + sums.shape[2:], F32)
    sums = lax.dynamic_update_slice_in_dim(empty, sums, core * own_blocks, axis=1)
    sums = lax.psum(sums, ("lat", "lon")) * (1.0 / math.sqrt(LATS * MODES))

    count = PARTS * blocks
    slots = count + DELAY * (chips - 1)
    slot_ids = jnp.arange(slots, dtype=jnp.int32)

    def place_of(late):
        v = slot_ids - DELAY * late
        return jnp.where((v >= 0) & (v < count), v, count)

    flat = jnp.zeros_like(slot_ids)
    scal = jnp.stack(
        [place_of(chip), place_of(chips - 1 - chip),
         flat + (chip == 0), flat + (chip == chips - 1)], axis=1
    ).astype(jnp.int32)
    sent = {}
    kept = None
    for t in range(slots):
        own, own_at = (spread[t // blocks], t % blocks) if t < count else (None, None)
        up, down, *kept = relay(
            t, scal, own, own_at, sent.pop(t - DELAY, None), kept, count,
            (coefs, row_block, half),
        )
        if t < count + DELAY * (chips - 2):
            sent[t] = (lax.ppermute(up, "lon", upward), lax.ppermute(down, "lon", downward))

    core_now = core.reshape(1).astype(jnp.int32)
    whole, for_other = to_grid(core_now, kept, panels, rows, width)
    field_gradient = place(core_now, lax.ppermute(for_other, "lon", swap), whole, row_block)
    return (field_gradient, sums[0], sums[1])


def solution(mesh):
    return jax.shard_map(
        local,
        mesh=mesh,
        in_specs=(P("lat", "lon", None), P("lat", "lon", None), P(), P()),
        out_specs=(P("lat", "lon", None), P(), P()),
        check_vma=False,
    )
```

```python
import functools
import math

import jax
import jax.numpy as jnp
from jax import lax
from jax.experimental import pallas as pl
from jax.experimental.pallas import tpu as pltpu
from jax.sharding import PartitionSpec as P

LATS = 448
LONS = 896
MODES = 128
BLOCKS = 8
BLOCK_W = 96
PARTS = 2
PIECES = 4
CHUNK = 8
EARLY = (-10, -8, -6, -4)
LATE = (5, 7, 9, 11)
DELAY = 2
LANES = 128
VMEM = 62 * 1024 * 1024
F32 = jnp.float32
BF16 = jnp.bfloat16


def trig_rows(row_ids, col_ids, period):
    phase = (row_ids[:, None] * col_ids[None, :] % period).astype(F32) * (2.0 * math.pi / period)
    factor = 1.0 / math.sqrt(period)
    return (
        (jnp.cos(phase) * factor).astype(BF16),
        (jnp.sin(phase) * factor).astype(BF16),
    )


def gelu_pair(value):
    cdf = 0.5 * (1.0 + lax.erf(value * 0.7071067811865476))
    density = jnp.exp(-0.5 * value * value) * 0.3989422804014327
    return (value * cdf, cdf + value * density)


def dot(left, right, left_dim=1, right_dim=0):
    return lax.dot_general(
        left, right, (((left_dim,), (right_dim,)), ((), ())), preferred_element_type=F32
    )


def params():
    return pltpu.CompilerParams(vmem_limit_bytes=VMEM)


def hop_body(t, row_block, has_recv, has_prev, has_final, ties, scal, *refs):
    refs = list(refs)
    fields, cot, fields_other, cot_other, tables = refs[:5]
    at = 5
    recv = refs[at : at + 2] if has_recv else None
    at += 2 * has_recv + has_prev + ties
    outs = refs[at : at + 2]
    at += 2
    final = None
    if has_final is not None:
        final = refs[at]
        at += 1
    x, table, recv_now, total, out, x_sem, table_sem, recv_sem, out_sem, final_sem = refs[at:]
    half = x.shape[-1]
    coefs = out.shape[1]
    tiles = half // LANES
    part_rows = row_block // 2
    mine = pl.ds(pl.multiple_of(scal[t, 6] * half, LANES), half)

    def row_copy(way, who, part, array):
        first = scal[t, 3 * way + 1] * row_block + part * part_rows
        rows = pl.ds(first, part_rows)
        source = array.at[rows] if who else array.at[rows, :, mine]
        return pltpu.make_async_copy(
            source, x.at[way, who, pl.ds(part * part_rows, part_rows)], x_sem.at[way, who, part]
        )

    def table_copy(way):
        source = tables.at[scal[t, 3 * way + 2], scal[t, 3 * way], 1 - way]
        return pltpu.make_async_copy(source, table.at[way], table_sem.at[way])

    def recv_copy(way):
        return pltpu.make_async_copy(recv[way], recv_now.at[way], recv_sem.at[way])

    def out_copy(way):
        return pltpu.make_async_copy(out.at[way], outs[way], out_sem.at[way])

    def final_copy(way):
        target = final.at[:, pl.ds(has_final * row_block, row_block), :]
        return pltpu.make_async_copy(out.at[way], target, final_sem)

    for way in range(2):
        table_copy(way).start()
        for part in range(2):
            for which, pair in enumerate(((fields, fields_other), (cot, cot_other))):
                @pl.when((scal[t, 3 * way] != 0) if which else (scal[t, 3 * way] == 0))
                def _(way=way, part=part, pair=pair):
                    for who in range(2):
                        row_copy(way, who, part, pair[who]).start()
        if has_recv:
            recv_copy(way).start()
    for way in range(2):
        table_copy(way).wait()
        for part in range(2):
            for who in range(2):
                row_copy(way, who, part, (fields, fields_other)[who]).wait()
            for h in range(part * part_rows, (part + 1) * part_rows):
                value = dot(table[way, 0], x[way, 0, h]) + dot(table[way, 1], x[way, 1, h])
                for j in range(tiles):
                    total[j, pl.ds(h, coefs, stride=row_block), :] = value[
                        :, j * LANES : (j + 1) * LANES
                    ]
        if has_recv:
            recv_copy(way).wait()
        for j in range(tiles):
            lanes = pl.ds(j * LANES, LANES)
            value = total[j].reshape(coefs, row_block, LANES)
            if has_recv:
                value = value + recv_now[way, :, :, lanes].astype(F32)
            out[way, :, :, lanes] = value.astype(BF16)
        out_copy(way).start()
    if has_final is not None:
        pl.when(scal[t, 7] == 0)(lambda: final_copy(1).start())
        pl.when(scal[t, 7] != 0)(lambda: final_copy(0).start())
    for way in range(2):
        out_copy(way).wait()
    if has_final is not None:
        final_copy(0).wait()


def hop(t, scal, arrays, tables, recv, prev, final_at, row_block, rows, ties=()):
    fields, _, fields_other, _ = arrays
    cols = fields.shape[1]
    half = fields_other.shape[2]
    coefs = tables.shape[4]
    operands = list(arrays) + [tables]
    if recv is not None:
        operands += list(recv)
    aliases = {}
    if prev is not None:
        aliases[1 + len(operands)] = 2
        operands.append(prev)
    operands += list(ties)
    out_shape = [jax.ShapeDtypeStruct((coefs, row_block, half), BF16)] * 2
    if final_at is not None:
        out_shape.append(jax.ShapeDtypeStruct((coefs, rows, half), BF16))
    anywhere = pl.BlockSpec(memory_space=pl.ANY)
    piece = pltpu.VMEM((2, coefs, row_block, half), BF16)
    return pl.pallas_call(
        functools.partial(
            hop_body, t, row_block, recv is not None, prev is not None, final_at, len(ties)
        ),
        grid_spec=pltpu.PrefetchScalarGridSpec(
            num_scalar_prefetch=1,
            grid=(),
            in_specs=[anywhere] * len(operands),
            out_specs=[anywhere] * len(out_shape),
            scratch_shapes=[
                pltpu.VMEM((2, 2, row_block, cols, half), BF16),
                pltpu.VMEM((2, 2, coefs, cols), BF16),
                piece,
                pltpu.VMEM((half // LANES, coefs * row_block, LANES), F32),
                piece,
                pltpu.SemaphoreType.DMA((2, 2, 2)),
                pltpu.SemaphoreType.DMA((2,)),
                pltpu.SemaphoreType.DMA((2,)),
                pltpu.SemaphoreType.DMA((2,)),
                pltpu.SemaphoreType.DMA,
            ],
        ),
        out_shape=out_shape,
        input_output_aliases=aliases,
        compiler_params=params(),
        cost_estimate=pl.CostEstimate(
            flops=8 * row_block * coefs * cols * half,
            bytes_accessed=16 * row_block * cols * half,
            transcendentals=0,
        ),
        name="longitude_hop",
    )(scal, *operands)


def filter_body(
    spectrum, pulled, forward, backward, inner, inner_t, outer_t,
    *refs,
):
    (adjoint, gradients, stack, z, back, hidden, u_adj, inner_total, outer_total) = refs[-9:]
    bands, _, _, rows, half = spectrum.shape
    lats = bands * rows
    tile = lats // 2

    @pl.when(pl.program_id(0) == 0)
    def _():
        inner_total[...] = jnp.zeros_like(inner_total)
        outer_total[...] = jnp.zeros_like(outer_total)

    for source, target in ((spectrum, z), (pulled, back)):
        for part in range(2):
            for band in range(bands):
                first = part * lats + band * rows
                stack[first : first + rows, :] = source[band, part, 0]
        for part in range(2):
            @pl.loop(0, 2)
            def _(i, part=part, target=target):
                at = pl.multiple_of(i * tile, 16)
                value = dot(forward[pl.ds(part * lats + at, tile), :], stack[...])
                target[pl.ds(at, tile), part * half : (part + 1) * half] = value.astype(BF16)

    @pl.loop(0, 2)
    def _(i):
        at = pl.ds(pl.multiple_of(i * tile, 16), tile)
        gelu, slope = gelu_pair(dot(z[at, :], inner[...]))
        hidden[at, :] = gelu.astype(BF16)
        u_adj[at, :] = (dot(back[at, :], outer_t[...]) * slope).astype(BF16)
        z_adj = dot(u_adj[at, :], inner_t[...]).astype(BF16)
        for part in range(2):
            where = pl.ds(pl.multiple_of(part * lats + i * tile, 16), tile)
            stack[where, :] = z_adj[:, part * half : (part + 1) * half]

    outer_total[...] += dot(hidden[...], back[...], 0, 0)
    inner_total[...] += dot(z[...], u_adj[...], 0, 0)
    for part in range(2):
        for band in range(bands):
            first = part * lats + band * rows
            value = dot(backward[first : first + rows, :], stack[...])
            adjoint[band, part, 0] = value.astype(BF16)

    @pl.when(pl.program_id(0) == pl.num_programs(0) - 1)
    def _():
        for which, total in enumerate((inner_total, outer_total)):
            for b in range(half // BLOCK_W):
                low = slice(b * BLOCK_W, (b + 1) * BLOCK_W)
                high = slice(half + b * BLOCK_W, half + (b + 1) * BLOCK_W)
                gradients[which, b, 0] = total[low, low] + total[high, high]
                gradients[which, b, 1] = total[low, high] - total[high, low]


def spectral_filter(first, modes, spectrum, pulled, forward, backward, inner, inner_t, outer_t, *ties):
    bands, _, _, rows, half = spectrum.shape
    lats = bands * rows
    wide = 2 * half
    data = pl.BlockSpec((bands, 2, 1, rows, half), lambda i: (0, 0, first + i, 0, 0))

    def whole(*shape):
        return pl.BlockSpec(shape, lambda i: (0,) * len(shape), pipeline_mode=pl.Buffered(1))

    square = whole(2 * lats, 2 * lats)
    weight = whole(wide, wide)
    gradients = (2, half // BLOCK_W, 2, BLOCK_W, BLOCK_W)
    return pl.pallas_call(
        filter_body,
        grid=(modes,),
        in_specs=[data, data, square, square, weight, weight, weight]
        + [pl.BlockSpec(memory_space=pl.ANY)] * len(ties),
        out_specs=[
            pl.BlockSpec((bands, 2, 1, rows, half), lambda i: (0, 0, i, 0, 0)),
            whole(*gradients),
        ],
        out_shape=[
            jax.ShapeDtypeStruct((bands, 2, modes, rows, half), BF16),
            jax.ShapeDtypeStruct(gradients, F32),
        ],
        scratch_shapes=[
            pltpu.VMEM((2 * lats, half), BF16),
            pltpu.VMEM((lats, wide), BF16),
            pltpu.VMEM((lats, wide), BF16),
            pltpu.VMEM((lats, wide), BF16),
            pltpu.VMEM((lats, wide), BF16),
            pltpu.VMEM((wide, wide), F32),
            pltpu.VMEM((wide, wide), F32),
        ],
        compiler_params=params(),
        cost_estimate=pl.CostEstimate(
            flops=modes * 2 * (3 * 4 * lats * lats * half + 5 * lats * wide * wide),
            bytes_accessed=6 * modes * 2 * lats * half,
            transcendentals=modes * 2 * lats * half * 2,
        ),
        name="spectral_filter",
    )(spectrum, pulled, forward, backward, inner, inner_t, outer_t, *ties)


def relay_body(t, has_own, has_recv, has_prev, ties, scal, *refs):
    refs = list(refs)
    own = refs.pop(0) if has_own else None
    recv = (refs.pop(0), refs.pop(0)) if has_recv else None
    refs = refs[2 * has_prev + ties :]
    sends, kept = refs[0:2], refs[2:4]
    for way in range(2):
        def put(value, way=way):
            sends[way][...] = value[...]
            kept[way][0] = value[...]

        if own is None:
            put(recv[way])
        elif recv is None:
            put(own)
        else:
            pl.when(scal[t, 2 + way] != 0)(functools.partial(put, own))
            pl.when(scal[t, 2 + way] == 0)(functools.partial(put, recv[way]))


def relay(t, scal, own, own_at, recv, prev, count, shape, ties=()):
    coefs, rows, half = shape
    piece = pl.BlockSpec(shape, lambda i, s: (0, 0, 0))
    in_specs, operands = [], []
    if own is not None:
        in_specs.append(pl.BlockSpec(shape, lambda i, s: (own_at, 0, 0)))
        operands.append(own)
    if recv is not None:
        in_specs += [piece, piece]
        operands += list(recv)
    aliases = {}
    if prev is not None:
        for i, array in enumerate(prev):
            aliases[1 + len(operands)] = 2 + i
            in_specs.append(pl.BlockSpec(memory_space=pl.ANY))
            operands.append(array)
    for array in ties:
        in_specs.append(pl.BlockSpec(memory_space=pl.ANY))
        operands.append(array)

    def kept(way):
        return pl.BlockSpec((1,) + shape, lambda i, s: (s[t, way], 0, 0, 0))

    return pl.pallas_call(
        functools.partial(
            relay_body, t, own is not None, recv is not None, prev is not None, len(ties)
        ),
        grid_spec=pltpu.PrefetchScalarGridSpec(
            num_scalar_prefetch=1,
            grid=(1,),
            in_specs=in_specs,
            out_specs=[piece, piece, kept(0), kept(1)],
        ),
        out_shape=[jax.ShapeDtypeStruct(shape, BF16)] * 2
        + [jax.ShapeDtypeStruct((count + 1,) + shape, BF16)] * 2,
        input_output_aliases=aliases,
        compiler_params=params(),
        cost_estimate=pl.CostEstimate(
            flops=0, bytes_accessed=8 * coefs * rows * half, transcendentals=0
        ),
        name="relay",
    )(scal, *operands)


def grid_body(core, *refs):
    pieces, panels, (own_out, other_out, *totals) = refs[:2], refs[2], refs[-4:]
    count, chunk, row_block, half = pieces[0].shape
    coefs = count * chunk
    tiles = half // LANES
    for total, piece in zip(totals, pieces):
        for j in range(tiles):
            value = piece[:, :, :, pl.ds(j * LANES, LANES)].astype(F32)
            total[j] = value.reshape(coefs * row_block, LANES)
    for h in range(row_block):
        rows = [
            jnp.concatenate(
                [total[j, pl.ds(h, coefs, stride=row_block), :] for j in range(tiles)], axis=1
            ).astype(BF16)
            for total in totals
        ]
        value = jnp.concatenate(rows, axis=0)
        own_out[h] = dot(panels[0], value).astype(BF16)
        other_out[h] = dot(panels[1], value).astype(BF16)


def to_grid(core, kept, panels, first, blocks, row_block, rows, width, whole, ties=()):
    count, chunk, _, half = kept[0].shape
    count -= 1
    cols = panels.shape[1]
    in_specs = [
        pl.BlockSpec((count, chunk, row_block, half), lambda i, s: (0, 0, first + i, 0))
    ] * 2 + [pl.BlockSpec(panels.shape, lambda i, s: (0, 0, 0))]
    operands = list(kept) + [panels]
    aliases = {}
    if whole is not None:
        aliases[1 + len(operands)] = 0
        ties = (whole,) + tuple(ties)
    for array in ties:
        in_specs.append(pl.BlockSpec(memory_space=pl.ANY))
        operands.append(array)
    total = pltpu.VMEM((half // LANES, count * chunk * row_block, LANES), F32)
    return pl.pallas_call(
        grid_body,
        grid_spec=pltpu.PrefetchScalarGridSpec(
            num_scalar_prefetch=1,
            grid=(blocks,),
            in_specs=in_specs,
            out_specs=[
                pl.BlockSpec((row_block, cols, half), lambda i, s: (first + i, 0, s[0])),
                pl.BlockSpec((row_block, cols, half), lambda i, s: (i, 0, 0)),
            ],
            scratch_shapes=[total] * 2,
        ),
        out_shape=[
            jax.ShapeDtypeStruct((rows, cols, width), BF16),
            jax.ShapeDtypeStruct((blocks * row_block, cols, half), BF16),
        ],
        input_output_aliases=aliases,
        compiler_params=params(),
        cost_estimate=pl.CostEstimate(
            flops=8 * blocks * row_block * count * chunk * cols * half,
            bytes_accessed=4 * (count * chunk + cols) * blocks * row_block * half,
            transcendentals=0,
        ),
        name="longitude_grid",
    )(core, *operands)


def place_body(core, piece, whole, out):
    out[...] = piece[...]


def place(core, piece, whole, first, row_block):
    rows, cols, half = piece.shape
    return pl.pallas_call(
        place_body,
        grid_spec=pltpu.PrefetchScalarGridSpec(
            num_scalar_prefetch=1,
            grid=(rows // row_block,),
            in_specs=[
                pl.BlockSpec((row_block, cols, half), lambda i, s: (i, 0, 0)),
                pl.BlockSpec(memory_space=pl.ANY),
            ],
            out_specs=pl.BlockSpec((row_block, cols, half), lambda i, s: (first + i, 0, 1 - s[0])),
        ),
        out_shape=jax.ShapeDtypeStruct(whole.shape, BF16),
        input_output_aliases={2: 0},
        compiler_params=params(),
        name="place",
    )(core, piece, whole)


def pick_body(core, array, *refs):
    out, sems = refs[-2:]
    rows, _, half = out.shape
    step = rows // sems.shape[0]
    lanes = pl.ds(pl.multiple_of((1 - core[0]) * half, LANES), half)
    copies = [
        pltpu.make_async_copy(
            array.at[pl.ds(i * step, step), :, lanes], out.at[pl.ds(i * step, step)], sems.at[i]
        )
        for i in range(sems.shape[0])
    ]
    for copy in copies:
        copy.start()
    for copy in copies:
        copy.wait()


def pick(core, array, rows, *ties):
    _, cols, width = array.shape
    anywhere = pl.BlockSpec(memory_space=pl.ANY)
    return pl.pallas_call(
        pick_body,
        grid_spec=pltpu.PrefetchScalarGridSpec(
            num_scalar_prefetch=1,
            grid=(),
            in_specs=[anywhere] * (1 + len(ties)),
            out_specs=anywhere,
            scratch_shapes=[pltpu.SemaphoreType.DMA((8,))],
        ),
        out_shape=jax.ShapeDtypeStruct((rows, cols, width // 2), BF16),
        compiler_params=params(),
        cost_estimate=pl.CostEstimate(
            flops=0, bytes_accessed=2 * rows * cols * width, transcendentals=0
        ),
        name="pick",
    )(core, array, *ties)


def block_diagonal(blocks):
    count, size, _ = blocks.shape
    eye = jnp.eye(count, dtype=blocks.dtype)
    wide = blocks[:, :, None, :] * eye[:, None, :, None]
    return wide.reshape(count * size, count * size)


def complex_weight(weight):
    real = block_diagonal(weight[:, 0])
    imag = block_diagonal(weight[:, 1])
    return jnp.concatenate(
        [
            jnp.concatenate([real, imag], axis=1),
            jnp.concatenate([-imag, real], axis=1),
        ],
        axis=0,
    )


def local(fields, cotangent, inner_weight, outer_weight):
    lat_count = lax.axis_size("lat")
    lon_count = lax.axis_size("lon")
    rows, cols, width = fields.shape
    chips = lon_count // 2
    half = width // 2
    lon = lax.axis_index("lon")
    chip = lon // 2
    core = lon % 2
    row_block = 16 if rows % 16 == 0 else 8
    blocks = rows // row_block
    per_end = MODES // 2
    per_group = per_end // lat_count
    per_part = per_group // PARTS
    coefs = lat_count * 2 * per_part
    swap = [(i, i ^ 1) for i in range(lon_count)]
    upward = [(i, i + 2) for i in range(lon_count - 2)]
    downward = [(i + 2, i) for i in range(lon_count - 2)]

    core_now = core.reshape(1).astype(jnp.int32)
    first_sent = pick(core_now, fields, DELAY * row_block)
    fields_sent = pick(core_now, fields, rows, first_sent)
    fields_first = lax.ppermute(first_sent, "lon", swap)
    fields_other = lax.ppermute(fields_sent, "lon", swap)
    cot_other = None

    q = jnp.arange(coefs, dtype=jnp.int32)
    part_of = q // per_part % 2
    ids = q // (2 * per_part) * per_group + q % per_part
    ends = jnp.arange(2, dtype=jnp.int32)[:, None, None] * per_end
    pieces = jnp.arange(PARTS, dtype=jnp.int32)[None, :, None] * per_part
    mode_ids = (ends + pieces + ids).reshape(-1)
    imag_row = jnp.tile(part_of, 2 * PARTS) == 1
    places = jnp.concatenate(
        [lon * cols + jnp.arange(cols, dtype=jnp.int32),
         (lon ^ 1) * cols + jnp.arange(cols, dtype=jnp.int32)]
    )
    cos_rows, sin_rows = trig_rows(mode_ids, places, LONS)
    per_piece = per_part // PIECES
    base = jnp.where(imag_row[:, None], -sin_rows, cos_rows)
    weights = jnp.where(mode_ids == 0, 1.0, 2.0).astype(BF16)
    both = jnp.stack([base, base * weights[:, None]], axis=0)
    tables = both.reshape(2, 2, PARTS, coefs, 2, cols).transpose(2, 0, 1, 4, 3, 5)
    panels = (
        base.reshape(2 * PARTS, 2 * lat_count, PIECES, per_piece, 2, cols)
        .transpose(4, 5, 0, 2, 1, 3)
        .reshape(2, cols, 2 * PARTS * coefs)
    )

    lat_ids = jnp.arange(LATS, dtype=jnp.int32)
    lat_cos, lat_sin = trig_rows(lat_ids, lat_ids, LATS)
    forward = jnp.concatenate(
        [jnp.concatenate([lat_cos, lat_sin], axis=1),
         jnp.concatenate([-lat_sin, lat_cos], axis=1)], axis=0
    )
    backward = jnp.concatenate(
        [jnp.concatenate([lat_cos, -lat_sin], axis=1),
         jnp.concatenate([lat_sin, lat_cos], axis=1)], axis=0
    )
    own_blocks = half // BLOCK_W
    inner = complex_weight(
        lax.dynamic_slice_in_dim(inner_weight, core * own_blocks, own_blocks, axis=0)
    )
    outer = complex_weight(
        lax.dynamic_slice_in_dim(outer_weight, core * own_blocks, own_blocks, axis=0)
    )
    inner_t, outer_t = inner.T, outer.T

    order = [(s, a, r) for s in range(PARTS) for a in range(2) for r in range(blocks)]
    count = len(order)
    slots = count + DELAY * (chips - 1)
    slot_ids = jnp.arange(slots, dtype=jnp.int32)

    def schedule(late):
        v = jnp.clip(slot_ids - DELAY * late, 0, count - 1)
        return [v // blocks % 2, v % blocks, v // (2 * blocks)]

    flat = jnp.zeros_like(slot_ids)
    scal = jnp.stack(
        schedule(chip) + schedule(chips - 1 - chip) + [flat + core, flat + chip], axis=1
    )
    def across(array):
        return lax.all_to_all(array, "lat", split_axis=0, concat_axis=0, tiled=True)

    spread = []
    gradients = 0.0

    def filter_piece(s, piece, *ties):
        nonlocal gradients
        shape = (lat_count, 2, per_part, rows, half)
        adjoint, part = spectral_filter(
            piece * per_piece, per_piece,
            every_row[s, 0].reshape(shape), every_row[s, 1].reshape(shape),
            forward, backward, inner, inner_t, outer_t, *ties,
        )
        gradients = gradients + part
        spread.append(across(adjoint.reshape(-1, rows, half)))
        return adjoint

    sent = {}
    gathered = {}
    every_row = {}
    for t in range(slots):
        v = t - DELAY * (chips - 1)
        if t < DELAY:
            arrays = (fields, fields, fields_first, fields_first)
        elif t < blocks:
            arrays = (fields, fields, fields_other, fields_other)
        else:
            arrays = (fields, cotangent, fields_other, cot_other)
        if t == DELAY:
            cot_other = lax.ppermute(pick(core_now, cotangent, rows, result[0]), "lon", swap)
        recv = sent.pop(t - DELAY, None)
        key, final_at, prev = None, None, None
        if v >= 0:
            key, final_at = order[v][:2], order[v][2]
            prev = gathered.get(key)
        ties = []
        if t - slots in EARLY:
            ties.append(filter_piece(0, EARLY.index(t - slots), result[0]))
        result = hop(t, scal, arrays, tables, recv, prev, final_at, row_block, rows, ties)
        if v >= 0:
            gathered[key] = result[2]
            if final_at == blocks - 1:
                every_row[key] = across(result[2])
        if t < count + DELAY * (chips - 2):
            sent[t] = (
                lax.ppermute(result[0], "lon", upward),
                lax.ppermute(result[1], "lon", downward),
            )
    def add_up(terms):
        at_end = (chip == 0) | (chip == chips - 1)
        terms = jnp.where(at_end, terms, 0.0).reshape(lat_count, -1, LANES)
        return jnp.sum(across(terms), axis=0)

    per_spread = coefs // (PIECES * CHUNK)
    count = PARTS * PIECES * per_spread
    slots = count + DELAY * (chips - 1)
    slot_ids = jnp.arange(slots, dtype=jnp.int32)

    def place_of(late):
        v = slot_ids - DELAY * late
        return jnp.where((v >= 0) & (v < count), v, count)

    flat = jnp.zeros_like(slot_ids)
    scal = jnp.stack(
        [place_of(chip), place_of(chips - 1 - chip),
         flat + (chip == 0), flat + (chip == chips - 1)], axis=1
    ).astype(jnp.int32)
    sent = {}
    kept = None
    for t in range(slots):
        own, own_at = (None, None)
        if t < count:
            own, own_at = spread[t // per_spread], t % per_spread
        ties = []
        if t in LATE:
            ties.append(filter_piece(1, LATE.index(t), up))
        if t == 0:
            ties.append(result[0])
        if t == LATE[-1] + 2:
            share = add_up(gradients)
            ties.append(share)
            by_core = lax.all_gather(share, "lon").reshape(chips, 2, -1, LANES)
            by_core = jnp.sum(by_core, axis=0)
            sums = lax.all_gather(by_core, "lat", axis=1, tiled=True)
        if t == slots - 1:
            ties.append(by_core)
        up, down, *kept = relay(
            t, scal, own, own_at, sent.pop(t - DELAY, None), kept, count,
            (CHUNK, rows, half), ties,
        )
        if t < count + DELAY * (chips - 2):
            sent[t] = (lax.ppermute(up, "lon", upward), lax.ppermute(down, "lon", downward))

    whole = None
    swapped = []
    for first, some in ((0, blocks - blocks // 2), (blocks - blocks // 2, blocks // 2)):
        whole, for_other = to_grid(
            core_now, kept, panels, first, some, row_block, rows, width, whole,
            (sums,) if first else (),
        )
        swapped.append((first, lax.ppermute(for_other, "lon", swap)))
    for first, piece in swapped:
        whole = place(core_now, piece, whole, first, row_block)
    sums = (sums * (1.0 / math.sqrt(LATS * MODES))).reshape(2, 2, own_blocks, 2, BLOCK_W, BLOCK_W)
    sums = jnp.swapaxes(sums, 0, 1).reshape(2, BLOCKS, 2, BLOCK_W, BLOCK_W)
    return (whole, sums[0], sums[1])


def solution(mesh):
    return jax.shard_map(
        local,
        mesh=mesh,
        in_specs=(P("lat", "lon", None), P("lat", "lon", None), P(), P()),
        out_specs=(P("lat", "lon", None), P(), P()),
        check_vma=False,
    )
```

```python
import functools
import math

import jax
import jax.numpy as jnp
from jax import lax
from jax.experimental import pallas as pl
from jax.experimental.pallas import tpu as pltpu
from jax.sharding import PartitionSpec as P

LATS = 448
LONS = 896
MODES = 128
BLOCKS = 8
BLOCK_W = 96
PARTS = 2
PIECES = 4
CHUNK = 8
DELAY = 2
LANES = 128
VMEM = 62 * 1024 * 1024
F32 = jnp.float32
BF16 = jnp.bfloat16


def trig_rows(row_ids, col_ids, period):
    phase = (row_ids[:, None] * col_ids[None, :] % period).astype(F32) * (2.0 * math.pi / period)
    factor = 1.0 / math.sqrt(period)
    return (
        (jnp.cos(phase) * factor).astype(BF16),
        (jnp.sin(phase) * factor).astype(BF16),
    )


def gelu_pair(value):
    cdf = 0.5 * (1.0 + lax.erf(value * 0.7071067811865476))
    density = jnp.exp(-0.5 * value * value) * 0.3989422804014327
    return (value * cdf, cdf + value * density)


def dot(left, right, left_dim=1, right_dim=0):
    return lax.dot_general(
        left, right, (((left_dim,), (right_dim,)), ((), ())), preferred_element_type=F32
    )


def params():
    return pltpu.CompilerParams(vmem_limit_bytes=VMEM)


def hop_body(t, row_block, has_recv, has_prev, has_final, ties, scal, *refs):
    refs = list(refs)
    fields, cot, fields_other, cot_other, tables = refs[:5]
    at = 5
    recv = refs[at : at + 2] if has_recv else None
    at += 2 * has_recv + has_prev + ties
    outs = refs[at : at + 2]
    at += 2
    final = None
    if has_final is not None:
        final = refs[at]
        at += 1
    x, table, recv_now, total, out, x_sem, table_sem, recv_sem, out_sem, final_sem = refs[at:]
    half = x.shape[-1]
    coefs = out.shape[1]
    tiles = half // LANES
    part_rows = row_block // 2
    mine = pl.ds(pl.multiple_of(scal[t, 6] * half, LANES), half)

    def row_copy(way, who, part, array):
        first = scal[t, 3 * way + 1] * row_block + part * part_rows
        rows = pl.ds(first, part_rows)
        source = array.at[rows] if who else array.at[rows, :, mine]
        return pltpu.make_async_copy(
            source, x.at[way, who, pl.ds(part * part_rows, part_rows)], x_sem.at[way, who, part]
        )

    def table_copy(way):
        source = tables.at[scal[t, 3 * way + 2], scal[t, 3 * way], 1 - way]
        return pltpu.make_async_copy(source, table.at[way], table_sem.at[way])

    def recv_copy(way):
        return pltpu.make_async_copy(recv[way], recv_now.at[way], recv_sem.at[way])

    def out_copy(way):
        return pltpu.make_async_copy(out.at[way], outs[way], out_sem.at[way])

    def final_copy(way):
        target = final.at[:, pl.ds(has_final * row_block, row_block), :]
        return pltpu.make_async_copy(out.at[way], target, final_sem)

    def fetch(way):
        table_copy(way).start()
        for part in range(2):
            for which, pair in enumerate(((fields, fields_other), (cot, cot_other))):
                @pl.when((scal[t, 3 * way] != 0) if which else (scal[t, 3 * way] == 0))
                def _(part=part, pair=pair):
                    for who in range(2):
                        row_copy(way, who, part, pair[who]).start()
        if has_recv:
            recv_copy(way).start()

    def work(way):
        table_copy(way).wait()
        for part in range(2):
            for who in range(2):
                row_copy(way, who, part, (fields, fields_other)[who]).wait()
            for h in range(part * part_rows, (part + 1) * part_rows):
                value = dot(table[way, 0], x[way, 0, h]) + dot(table[way, 1], x[way, 1, h])
                for j in range(tiles):
                    total[j, pl.ds(h, coefs, stride=row_block), :] = value[
                        :, j * LANES : (j + 1) * LANES
                    ]
        if has_recv:
            recv_copy(way).wait()
        for j in range(tiles):
            lanes = pl.ds(j * LANES, LANES)
            value = total[j].reshape(coefs, row_block, LANES)
            if has_recv:
                value = value + recv_now[way, :, :, lanes].astype(F32)
            out[way, :, :, lanes] = value.astype(BF16)
        out_copy(way).start()

    for step in (fetch, work):
        for way in range(2):
            pl.when(scal[t, 8 + way] != 0)(functools.partial(step, way))
    if has_final is not None:
        pl.when(scal[t, 7] == 0)(lambda: final_copy(1).start())
        pl.when(scal[t, 7] != 0)(lambda: final_copy(0).start())
    for way in range(2):
        pl.when(scal[t, 8 + way] != 0)(lambda way=way: out_copy(way).wait())
    if has_final is not None:
        final_copy(0).wait()


def hop(t, scal, arrays, tables, recv, prev, final_at, row_block, rows, ties=()):
    fields, _, fields_other, _ = arrays
    cols = fields.shape[1]
    half = fields_other.shape[2]
    coefs = tables.shape[4]
    operands = list(arrays) + [tables]
    if recv is not None:
        operands += list(recv)
    aliases = {}
    if prev is not None:
        aliases[1 + len(operands)] = 2
        operands.append(prev)
    operands += list(ties)
    out_shape = [jax.ShapeDtypeStruct((coefs, row_block, half), BF16)] * 2
    if final_at is not None:
        out_shape.append(jax.ShapeDtypeStruct((coefs, rows, half), BF16))
    anywhere = pl.BlockSpec(memory_space=pl.ANY)
    piece = pltpu.VMEM((2, coefs, row_block, half), BF16)
    return pl.pallas_call(
        functools.partial(
            hop_body, t, row_block, recv is not None, prev is not None, final_at, len(ties)
        ),
        grid_spec=pltpu.PrefetchScalarGridSpec(
            num_scalar_prefetch=1,
            grid=(),
            in_specs=[anywhere] * len(operands),
            out_specs=[anywhere] * len(out_shape),
            scratch_shapes=[
                pltpu.VMEM((2, 2, row_block, cols, half), BF16),
                pltpu.VMEM((2, 2, coefs, cols), BF16),
                piece,
                pltpu.VMEM((half // LANES, coefs * row_block, LANES), F32),
                piece,
                pltpu.SemaphoreType.DMA((2, 2, 2)),
                pltpu.SemaphoreType.DMA((2,)),
                pltpu.SemaphoreType.DMA((2,)),
                pltpu.SemaphoreType.DMA((2,)),
                pltpu.SemaphoreType.DMA,
            ],
        ),
        out_shape=out_shape,
        input_output_aliases=aliases,
        compiler_params=params(),
        cost_estimate=pl.CostEstimate(
            flops=8 * row_block * coefs * cols * half,
            bytes_accessed=16 * row_block * cols * half,
            transcendentals=0,
        ),
        name="longitude_hop",
    )(scal, *operands)


def filter_body(
    spectrum, pulled, forward, backward, inner, inner_t, outer_t,
    *refs,
):
    (adjoint, gradients, stack, z, back, hidden, u_adj, inner_total, outer_total) = refs[-9:]
    bands, _, _, rows, half = spectrum.shape
    lats = bands * rows
    tile = lats // 2

    @pl.when(pl.program_id(0) == 0)
    def _():
        inner_total[...] = jnp.zeros_like(inner_total)
        outer_total[...] = jnp.zeros_like(outer_total)

    for source, target in ((spectrum, z), (pulled, back)):
        for part in range(2):
            for band in range(bands):
                first = part * lats + band * rows
                stack[first : first + rows, :] = source[band, part, 0]
        for part in range(2):
            @pl.loop(0, 2)
            def _(i, part=part, target=target):
                at = pl.multiple_of(i * tile, 16)
                value = dot(forward[pl.ds(part * lats + at, tile), :], stack[...])
                target[pl.ds(at, tile), part * half : (part + 1) * half] = value.astype(BF16)

    @pl.loop(0, 2)
    def _(i):
        at = pl.ds(pl.multiple_of(i * tile, 16), tile)
        gelu, slope = gelu_pair(dot(z[at, :], inner[...]))
        hidden[at, :] = gelu.astype(BF16)
        u_adj[at, :] = (dot(back[at, :], outer_t[...]) * slope).astype(BF16)
        z_adj = dot(u_adj[at, :], inner_t[...]).astype(BF16)
        for part in range(2):
            where = pl.ds(pl.multiple_of(part * lats + i * tile, 16), tile)
            stack[where, :] = z_adj[:, part * half : (part + 1) * half]

    outer_total[...] += dot(hidden[...], back[...], 0, 0)
    inner_total[...] += dot(z[...], u_adj[...], 0, 0)
    for part in range(2):
        for band in range(bands):
            first = part * lats + band * rows
            value = dot(backward[first : first + rows, :], stack[...])
            adjoint[band, part, 0] = value.astype(BF16)

    @pl.when(pl.program_id(0) == pl.num_programs(0) - 1)
    def _():
        for which, total in enumerate((inner_total, outer_total)):
            for b in range(half // BLOCK_W):
                low = slice(b * BLOCK_W, (b + 1) * BLOCK_W)
                high = slice(half + b * BLOCK_W, half + (b + 1) * BLOCK_W)
                gradients[which, b, 0] = total[low, low] + total[high, high]
                gradients[which, b, 1] = total[low, high] - total[high, low]


def spectral_filter(first, modes, spectrum, pulled, forward, backward, inner, inner_t, outer_t, *ties):
    bands, _, _, rows, half = spectrum.shape
    lats = bands * rows
    wide = 2 * half
    data = pl.BlockSpec((bands, 2, 1, rows, half), lambda i: (0, 0, first + i, 0, 0))

    def whole(*shape):
        return pl.BlockSpec(shape, lambda i: (0,) * len(shape), pipeline_mode=pl.Buffered(1))

    square = whole(2 * lats, 2 * lats)
    weight = whole(wide, wide)
    gradients = (2, half // BLOCK_W, 2, BLOCK_W, BLOCK_W)
    return pl.pallas_call(
        filter_body,
        grid=(modes,),
        in_specs=[data, data, square, square, weight, weight, weight]
        + [pl.BlockSpec(memory_space=pl.ANY)] * len(ties),
        out_specs=[
            pl.BlockSpec((bands, 2, 1, rows, half), lambda i: (0, 0, i, 0, 0)),
            whole(*gradients),
        ],
        out_shape=[
            jax.ShapeDtypeStruct((bands, 2, modes, rows, half), BF16),
            jax.ShapeDtypeStruct(gradients, F32),
        ],
        scratch_shapes=[
            pltpu.VMEM((2 * lats, half), BF16),
            pltpu.VMEM((lats, wide), BF16),
            pltpu.VMEM((lats, wide), BF16),
            pltpu.VMEM((lats, wide), BF16),
            pltpu.VMEM((lats, wide), BF16),
            pltpu.VMEM((wide, wide), F32),
            pltpu.VMEM((wide, wide), F32),
        ],
        compiler_params=params(),
        cost_estimate=pl.CostEstimate(
            flops=modes * 2 * (3 * 4 * lats * lats * half + 5 * lats * wide * wide),
            bytes_accessed=6 * modes * 2 * lats * half,
            transcendentals=modes * 2 * lats * half * 2,
        ),
        name="spectral_filter",
    )(spectrum, pulled, forward, backward, inner, inner_t, outer_t, *ties)


def relay_body(t, has_own, has_recv, has_prev, ties, scal, *refs):
    refs = list(refs)
    own = refs.pop(0) if has_own else None
    recv = (refs.pop(0), refs.pop(0)) if has_recv else None
    refs = refs[2 * has_prev + ties :]
    sends, kept = refs[0:2], refs[2:4]
    for way in range(2):
        def put(value, way=way):
            sends[way][...] = value[...]
            kept[way][0] = value[...]

        if own is None:
            put(recv[way])
        elif recv is None:
            put(own)
        else:
            pl.when(scal[t, 2 + way] != 0)(functools.partial(put, own))
            pl.when(scal[t, 2 + way] == 0)(functools.partial(put, recv[way]))


def relay(t, scal, own, own_at, recv, prev, count, shape, ties=()):
    coefs, rows, half = shape
    piece = pl.BlockSpec(shape, lambda i, s: (0, 0, 0))
    in_specs, operands = [], []
    if own is not None:
        in_specs.append(pl.BlockSpec(shape, lambda i, s: (own_at, 0, 0)))
        operands.append(own)
    if recv is not None:
        in_specs += [piece, piece]
        operands += list(recv)
    aliases = {}
    if prev is not None:
        for i, array in enumerate(prev):
            aliases[1 + len(operands)] = 2 + i
            in_specs.append(pl.BlockSpec(memory_space=pl.ANY))
            operands.append(array)
    for array in ties:
        in_specs.append(pl.BlockSpec(memory_space=pl.ANY))
        operands.append(array)

    def kept(way):
        return pl.BlockSpec((1,) + shape, lambda i, s: (s[t, way], 0, 0, 0))

    return pl.pallas_call(
        functools.partial(
            relay_body, t, own is not None, recv is not None, prev is not None, len(ties)
        ),
        grid_spec=pltpu.PrefetchScalarGridSpec(
            num_scalar_prefetch=1,
            grid=(1,),
            in_specs=in_specs,
            out_specs=[piece, piece, kept(0), kept(1)],
        ),
        out_shape=[jax.ShapeDtypeStruct(shape, BF16)] * 2
        + [jax.ShapeDtypeStruct((count + 1,) + shape, BF16)] * 2,
        input_output_aliases=aliases,
        compiler_params=params(),
        cost_estimate=pl.CostEstimate(
            flops=0, bytes_accessed=8 * coefs * rows * half, transcendentals=0
        ),
        name="relay",
    )(scal, *operands)


def grid_body(core, *refs):
    pieces, panels, (own_out, other_out, *totals) = refs[:2], refs[2], refs[-4:]
    count, chunk, row_block, half = pieces[0].shape
    coefs = count * chunk
    tiles = half // LANES
    for total, piece in zip(totals, pieces):
        for j in range(tiles):
            value = piece[:, :, :, pl.ds(j * LANES, LANES)].astype(F32)
            total[j] = value.reshape(coefs * row_block, LANES)
    for h in range(row_block):
        rows = [
            jnp.concatenate(
                [total[j, pl.ds(h, coefs, stride=row_block), :] for j in range(tiles)], axis=1
            ).astype(BF16)
            for total in totals
        ]
        value = jnp.concatenate(rows, axis=0)
        own_out[h] = dot(panels[0], value).astype(BF16)
        other_out[h] = dot(panels[1], value).astype(BF16)


def to_grid(core, kept, panels, first, blocks, row_block, rows, width, whole, ties=()):
    count, chunk, _, half = kept[0].shape
    count -= 1
    cols = panels.shape[1]
    in_specs = [
        pl.BlockSpec((count, chunk, row_block, half), lambda i, s: (0, 0, first + i, 0))
    ] * 2 + [pl.BlockSpec(panels.shape, lambda i, s: (0, 0, 0))]
    operands = list(kept) + [panels]
    aliases = {}
    if whole is not None:
        aliases[1 + len(operands)] = 0
        ties = (whole,) + tuple(ties)
    for array in ties:
        in_specs.append(pl.BlockSpec(memory_space=pl.ANY))
        operands.append(array)
    total = pltpu.VMEM((half // LANES, count * chunk * row_block, LANES), F32)
    return pl.pallas_call(
        grid_body,
        grid_spec=pltpu.PrefetchScalarGridSpec(
            num_scalar_prefetch=1,
            grid=(blocks,),
            in_specs=in_specs,
            out_specs=[
                pl.BlockSpec((row_block, cols, half), lambda i, s: (first + i, 0, s[0])),
                pl.BlockSpec((row_block, cols, half), lambda i, s: (i, 0, 0)),
            ],
            scratch_shapes=[total] * 2,
        ),
        out_shape=[
            jax.ShapeDtypeStruct((rows, cols, width), BF16),
            jax.ShapeDtypeStruct((blocks * row_block, cols, half), BF16),
        ],
        input_output_aliases=aliases,
        compiler_params=params(),
        cost_estimate=pl.CostEstimate(
            flops=8 * blocks * row_block * count * chunk * cols * half,
            bytes_accessed=4 * (count * chunk + cols) * blocks * row_block * half,
            transcendentals=0,
        ),
        name="longitude_grid",
    )(core, *operands)


def place_body(core, piece, whole, out):
    out[...] = piece[...]


def place(core, piece, whole, first, row_block):
    rows, cols, half = piece.shape
    return pl.pallas_call(
        place_body,
        grid_spec=pltpu.PrefetchScalarGridSpec(
            num_scalar_prefetch=1,
            grid=(rows // row_block,),
            in_specs=[
                pl.BlockSpec((row_block, cols, half), lambda i, s: (i, 0, 0)),
                pl.BlockSpec(memory_space=pl.ANY),
            ],
            out_specs=pl.BlockSpec((row_block, cols, half), lambda i, s: (first + i, 0, 1 - s[0])),
        ),
        out_shape=jax.ShapeDtypeStruct(whole.shape, BF16),
        input_output_aliases={2: 0},
        compiler_params=params(),
        name="place",
    )(core, piece, whole)


def pick_body(core, array, *refs):
    refs[-1][...] = array[...]


def pick(core, array, rows, row_block, *ties):
    _, cols, width = array.shape
    half = width // 2
    anywhere = pl.BlockSpec(memory_space=pl.ANY)
    return pl.pallas_call(
        pick_body,
        grid_spec=pltpu.PrefetchScalarGridSpec(
            num_scalar_prefetch=1,
            grid=(rows // row_block,),
            in_specs=[pl.BlockSpec((row_block, cols, half), lambda i, s: (i, 0, 1 - s[0]))]
            + [anywhere] * len(ties),
            out_specs=pl.BlockSpec((row_block, cols, half), lambda i, s: (i, 0, 0)),
        ),
        out_shape=jax.ShapeDtypeStruct((rows, cols, half), BF16),
        compiler_params=params(),
        cost_estimate=pl.CostEstimate(
            flops=0, bytes_accessed=2 * rows * cols * width, transcendentals=0
        ),
        name="pick",
    )(core, array, *ties)


def block_diagonal(blocks):
    count, size, _ = blocks.shape
    eye = jnp.eye(count, dtype=blocks.dtype)
    wide = blocks[:, :, None, :] * eye[:, None, :, None]
    return wide.reshape(count * size, count * size)


def complex_weight(weight):
    real = block_diagonal(weight[:, 0])
    imag = block_diagonal(weight[:, 1])
    return jnp.concatenate(
        [
            jnp.concatenate([real, imag], axis=1),
            jnp.concatenate([-imag, real], axis=1),
        ],
        axis=0,
    )


def local(fields, cotangent, inner_weight, outer_weight):
    lat_count = lax.axis_size("lat")
    lon_count = lax.axis_size("lon")
    rows, cols, width = fields.shape
    chips = lon_count // 2
    half = width // 2
    lon = lax.axis_index("lon")
    chip = lon // 2
    core = lon % 2
    row_block = 16 if rows % 16 == 0 else 8
    blocks = rows // row_block
    per_end = MODES // 2
    per_group = per_end // lat_count
    per_part = per_group // PARTS
    coefs = lat_count * 2 * per_part
    swap = [(i, i ^ 1) for i in range(lon_count)]
    upward = [(i, i + 2) for i in range(lon_count - 2)]
    downward = [(i + 2, i) for i in range(lon_count - 2)]

    core_now = core.reshape(1).astype(jnp.int32)
    first_sent = pick(core_now, fields, DELAY * row_block, row_block)
    fields_sent = pick(core_now, fields, rows, row_block, first_sent)
    fields_first = lax.ppermute(first_sent, "lon", swap)
    fields_other = lax.ppermute(fields_sent, "lon", swap)
    cot_other = None

    q = jnp.arange(coefs, dtype=jnp.int32)
    part_of = q // per_part % 2
    ids = q // (2 * per_part) * per_group + q % per_part
    ends = jnp.arange(2, dtype=jnp.int32)[:, None, None] * per_end
    pieces = jnp.arange(PARTS, dtype=jnp.int32)[None, :, None] * per_part
    mode_ids = (ends + pieces + ids).reshape(-1)
    imag_row = jnp.tile(part_of, 2 * PARTS) == 1
    places = jnp.concatenate(
        [lon * cols + jnp.arange(cols, dtype=jnp.int32),
         (lon ^ 1) * cols + jnp.arange(cols, dtype=jnp.int32)]
    )
    cos_rows, sin_rows = trig_rows(mode_ids, places, LONS)
    per_piece = per_part // PIECES
    base = jnp.where(imag_row[:, None], -sin_rows, cos_rows)
    weights = jnp.where(mode_ids == 0, 1.0, 2.0).astype(BF16)
    both = jnp.stack([base, base * weights[:, None]], axis=0)
    tables = both.reshape(2, 2, PARTS, coefs, 2, cols).transpose(2, 0, 1, 4, 3, 5)
    panels = (
        base.reshape(2 * PARTS, 2 * lat_count, PIECES, per_piece, 2, cols)
        .transpose(4, 5, 0, 2, 1, 3)
        .reshape(2, cols, 2 * PARTS * coefs)
    )

    lat_ids = jnp.arange(LATS, dtype=jnp.int32)
    lat_cos, lat_sin = trig_rows(lat_ids, lat_ids, LATS)
    forward = jnp.concatenate(
        [jnp.concatenate([lat_cos, lat_sin], axis=1),
         jnp.concatenate([-lat_sin, lat_cos], axis=1)], axis=0
    )
    backward = jnp.concatenate(
        [jnp.concatenate([lat_cos, -lat_sin], axis=1),
         jnp.concatenate([lat_sin, lat_cos], axis=1)], axis=0
    )
    own_blocks = half // BLOCK_W
    inner = complex_weight(
        lax.dynamic_slice_in_dim(inner_weight, core * own_blocks, own_blocks, axis=0)
    )
    outer = complex_weight(
        lax.dynamic_slice_in_dim(outer_weight, core * own_blocks, own_blocks, axis=0)
    )
    inner_t, outer_t = inner.T, outer.T

    order = [(s, a, r) for s in range(PARTS) for a in range(2) for r in range(blocks)]
    count = len(order)
    slots = count + DELAY * (chips - 1)
    slot_ids = jnp.arange(slots, dtype=jnp.int32)

    def schedule(late):
        v = jnp.clip(slot_ids - DELAY * late, 0, count - 1)
        return [v // blocks % 2, v % blocks, v // (2 * blocks)]

    def has_chunk(late):
        v = slot_ids - DELAY * late
        return ((v >= 0) & (v < count)).astype(jnp.int32)

    flat = jnp.zeros_like(slot_ids)
    hop_plan = jnp.stack(
        schedule(chip)
        + schedule(chips - 1 - chip)
        + [flat + core, flat + chip, has_chunk(chip), has_chunk(chips - 1 - chip)],
        axis=1,
    )
    def across(array):
        return lax.all_to_all(array, "lat", split_axis=0, concat_axis=0, tiled=True)

    last = []
    sent, gathered, every_row, spread, terms = {}, {}, {}, [], []
    others = {"cot": None}

    def hop_slot(t):
        v = t - DELAY * (chips - 1)
        if t < DELAY:
            arrays = (fields, fields, fields_first, fields_first)
        elif t < blocks:
            arrays = (fields, fields, fields_other, fields_other)
        else:
            arrays = (fields, cotangent, fields_other, others["cot"])
        recv = sent.pop(t - DELAY, None)
        key, final_at, prev = None, None, None
        if v >= 0:
            key, final_at = order[v][:2], order[v][2]
            prev = gathered.get(key)
        result = hop(t, hop_plan, arrays, tables, recv, prev, final_at, row_block, rows, last)
        last[:] = [result[0]]
        if v >= 0:
            gathered[key] = result[2]
            if final_at == blocks - 1:
                every_row[key] = across(result[2])
        if t < count + DELAY * (chips - 2):
            sent[t] = (
                lax.ppermute(result[0], "lon", upward),
                lax.ppermute(result[1], "lon", downward),
            )
        if t == DELAY - 1:
            cot_sent = pick(core_now, cotangent, rows, row_block, *last)
            last[:] = [cot_sent]
            others["cot"] = lax.ppermute(cot_sent, "lon", swap)

    def filter_piece(n):
        s, piece = n // PIECES, n % PIECES
        shape = (lat_count, 2, per_part, rows, half)
        adjoint, part = spectral_filter(
            piece * per_piece, per_piece,
            every_row[s, 0].reshape(shape), every_row[s, 1].reshape(shape),
            forward, backward, inner, inner_t, outer_t, *last,
        )
        last[:] = [adjoint]
        terms.append(part)
        spread.append(across(adjoint.reshape(-1, rows, half)))

    def add_up():
        at_end = (chip == 0) | (chip == chips - 1)
        now = jnp.where(at_end, sum(terms), 0.0).reshape(lat_count, -1, LANES)
        return jnp.sum(across(now), axis=0)

    per_spread = coefs // (PIECES * CHUNK)
    relay_count = PARTS * PIECES * per_spread
    relay_slots = relay_count + DELAY * (chips - 1)
    relay_ids = jnp.arange(relay_slots, dtype=jnp.int32)

    def place_of(late):
        v = relay_ids - DELAY * late
        return jnp.where((v >= 0) & (v < relay_count), v, relay_count)

    flat = jnp.zeros_like(relay_ids)
    relay_plan = jnp.stack(
        [place_of(chip), place_of(chips - 1 - chip),
         flat + (chip == 0), flat + (chip == chips - 1)], axis=1
    ).astype(jnp.int32)
    passed = {}
    kept = []

    def relay_slot(t, *ties):
        own, own_at = (None, None)
        if t < relay_count:
            own, own_at = spread[t // per_spread], t % per_spread
        up, down, *kept[:] = relay(
            t, relay_plan, own, own_at, passed.pop(t - DELAY, None), tuple(kept) or None,
            relay_count, (CHUNK, rows, half), last + list(ties),
        )
        last[:] = [up]
        if t < relay_count + DELAY * (chips - 2):
            passed[t] = (lax.ppermute(up, "lon", upward), lax.ppermute(down, "lon", downward))

    for t in range(slots):
        if t in (slots - 9, slots - 6):
            filter_piece(len(spread))
        hop_slot(t)
        if slots - 6 <= t < slots - 2:
            relay_slot(t - slots + 6)
    filter_piece(2)
    filter_piece(3)
    for t in range(4, relay_slots):
        if t in (7, 8, 10, 12):
            filter_piece(len(spread))
        ties = []
        if t == 13:
            share = add_up()
            ties.append(share)
            by_core = lax.all_gather(share, "lon").reshape(chips, 2, -1, LANES)
            by_core = jnp.sum(by_core, axis=0)
            sums = lax.all_gather(by_core, "lat", axis=1, tiled=True)
        if t == relay_slots - 1:
            ties.append(by_core)
        relay_slot(t, *ties)

    whole = None
    swapped = []
    for first, some in ((0, blocks - blocks // 2), (blocks - blocks // 2, blocks // 2)):
        whole, for_other = to_grid(
            core_now, kept, panels, first, some, row_block, rows, width, whole,
            (sums,) if first else (),
        )
        swapped.append((first, lax.ppermute(for_other, "lon", swap)))
    for first, piece in swapped:
        whole = place(core_now, piece, whole, first, row_block)
    sums = (sums * (1.0 / math.sqrt(LATS * MODES))).reshape(2, 2, own_blocks, 2, BLOCK_W, BLOCK_W)
    sums = jnp.swapaxes(sums, 0, 1).reshape(2, BLOCKS, 2, BLOCK_W, BLOCK_W)
    return (whole, sums[0], sums[1])


def solution(mesh):
    return jax.shard_map(
        local,
        mesh=mesh,
        in_specs=(P("lat", "lon", None), P("lat", "lon", None), P(), P()),
        out_specs=(P("lat", "lon", None), P(), P()),
        check_vma=False,
    )
```

```python
import functools
import math

import jax
import jax.numpy as jnp
from jax import lax
from jax.experimental import pallas as pl
from jax.experimental.pallas import tpu as pltpu
from jax.sharding import PartitionSpec as P

LATS = 448
LONS = 896
MODES = 128
BLOCKS = 8
BLOCK_W = 96
PARTS = 4
CHUNK = 8
FIRST = 3
DELAY = 2
LANES = 128
VMEM = 62 * 1024 * 1024
F32 = jnp.float32
BF16 = jnp.bfloat16


def trig_rows(row_ids, col_ids, period):
    phase = (row_ids[:, None] * col_ids[None, :] % period).astype(F32) * (2.0 * math.pi / period)
    factor = 1.0 / math.sqrt(period)
    return (
        (jnp.cos(phase) * factor).astype(BF16),
        (jnp.sin(phase) * factor).astype(BF16),
    )


def gelu_pair(value):
    cdf = 0.5 * (1.0 + lax.erf(value * 0.7071067811865476))
    density = jnp.exp(-0.5 * value * value) * 0.3989422804014327
    return (value * cdf, cdf + value * density)


def dot(left, right, left_dim=1, right_dim=0):
    return lax.dot_general(
        left, right, (((left_dim,), (right_dim,)), ((), ())), preferred_element_type=F32
    )


def params():
    return pltpu.CompilerParams(vmem_limit_bytes=VMEM)


def hop_body(t, bands, row_block, has_recv, has_prev, has_final, ties, scal, *refs):
    refs = list(refs)
    fields, cot, fields_other, cot_other, tables = refs[:5]
    at = 5
    recv = refs[at : at + 2] if has_recv else None
    at += 2 * has_recv + has_prev + ties
    outs = refs[at : at + 2]
    at += 2
    final = None
    if has_final is not None:
        final = refs[at]
        at += 1
    x, table, recv_now, total, out, x_sem, table_sem, recv_sem, out_sem, final_sem = refs[at:]
    half = x.shape[-1]
    coefs = out.shape[1]
    share = coefs // (2 * bands)
    tiles = half // LANES
    mine = pl.ds(pl.multiple_of(scal[t, 4] * half, LANES), half)

    def row_copy(way, which, who):
        rows = pl.ds(scal[t, 2 * way] * row_block, row_block)
        array = ((fields, fields_other), (cot, cot_other))[which][who]
        source = array.at[rows] if who else array.at[rows, :, mine]
        return pltpu.make_async_copy(source, x.at[way, which, who], x_sem.at[way, which, who])

    def table_copy(way):
        source = tables.at[scal[t, 2 * way + 1], 1 - way]
        return pltpu.make_async_copy(source, table.at[way], table_sem.at[way])

    def recv_copy(way):
        return pltpu.make_async_copy(recv[way], recv_now.at[way], recv_sem.at[way])

    def out_copy(way):
        return pltpu.make_async_copy(out.at[way], outs[way], out_sem.at[way])

    def final_copy(way):
        target = final.at[:, pl.ds(has_final * row_block, row_block), :]
        return pltpu.make_async_copy(out.at[way], target, final_sem)

    def fetch(way):
        table_copy(way).start()
        for which in range(2):
            for who in range(2):
                row_copy(way, which, who).start()
        if has_recv:
            recv_copy(way).start()

    def work(way):
        table_copy(way).wait()
        for which in range(2):
            for who in range(2):
                row_copy(way, which, who).wait()
            for h in range(row_block):
                value = dot(table[way, which, 0], x[way, which, 0, h])
                value = value + dot(table[way, which, 1], x[way, which, 1, h])
                for band in range(bands):
                    first = (2 * band + which) * share * row_block + h
                    for j in range(tiles):
                        total[j, pl.ds(first, share, stride=row_block), :] = value[
                            band * share : (band + 1) * share, j * LANES : (j + 1) * LANES
                        ]
        if has_recv:
            recv_copy(way).wait()
        for j in range(tiles):
            lanes = pl.ds(j * LANES, LANES)
            value = total[j].reshape(coefs, row_block, LANES)
            if has_recv:
                value = value + recv_now[way, :, :, lanes].astype(F32)
            out[way, :, :, lanes] = value.astype(BF16)
        out_copy(way).start()

    for step in (fetch, work):
        for way in range(2):
            pl.when(scal[t, 6 + way] != 0)(functools.partial(step, way))
    if has_final is not None:
        pl.when(scal[t, 5] == 0)(lambda: final_copy(1).start())
        pl.when(scal[t, 5] != 0)(lambda: final_copy(0).start())
    for way in range(2):
        pl.when(scal[t, 6 + way] != 0)(lambda way=way: out_copy(way).wait())
    if has_final is not None:
        final_copy(0).wait()


def hop(t, bands, scal, arrays, tables, recv, prev, final_at, row_block, rows, ties=()):
    fields, _, fields_other, _ = arrays
    cols = fields.shape[1]
    half = fields_other.shape[2]
    coefs = 2 * tables.shape[4]
    operands = list(arrays) + [tables]
    if recv is not None:
        operands += list(recv)
    aliases = {}
    if prev is not None:
        aliases[1 + len(operands)] = 2
        operands.append(prev)
    operands += list(ties)
    out_shape = [jax.ShapeDtypeStruct((coefs, row_block, half), BF16)] * 2
    if final_at is not None:
        out_shape.append(jax.ShapeDtypeStruct((coefs, rows, half), BF16))
    anywhere = pl.BlockSpec(memory_space=pl.ANY)
    piece = pltpu.VMEM((2, coefs, row_block, half), BF16)
    return pl.pallas_call(
        functools.partial(
            hop_body, t, bands, row_block, recv is not None, prev is not None, final_at, len(ties)
        ),
        grid_spec=pltpu.PrefetchScalarGridSpec(
            num_scalar_prefetch=1,
            grid=(),
            in_specs=[anywhere] * len(operands),
            out_specs=[anywhere] * len(out_shape),
            scratch_shapes=[
                pltpu.VMEM((2, 2, 2, row_block, cols, half), BF16),
                pltpu.VMEM((2,) + tables.shape[2:], BF16),
                piece,
                pltpu.VMEM((half // LANES, coefs * row_block, LANES), F32),
                piece,
                pltpu.SemaphoreType.DMA((2, 2, 2)),
                pltpu.SemaphoreType.DMA((2,)),
                pltpu.SemaphoreType.DMA((2,)),
                pltpu.SemaphoreType.DMA((2,)),
                pltpu.SemaphoreType.DMA,
            ],
        ),
        out_shape=out_shape,
        input_output_aliases=aliases,
        compiler_params=params(),
        cost_estimate=pl.CostEstimate(
            flops=8 * row_block * coefs * cols * half,
            bytes_accessed=24 * row_block * cols * half,
            transcendentals=0,
        ),
        name="longitude_hop",
    )(scal, *operands)


def filter_body(
    data, forward, backward, inner, inner_t, outer_t, *refs,
):
    (adjoint, gradients, stack, z, back, hidden, u_adj, inner_total, outer_total) = refs[-9:]
    bands, _, _, _, rows, half = data.shape
    lats = bands * rows
    tile = lats // 2

    @pl.when(pl.program_id(0) == 0)
    def _():
        inner_total[...] = jnp.zeros_like(inner_total)
        outer_total[...] = jnp.zeros_like(outer_total)

    for which, target in enumerate((z, back)):
        for part in range(2):
            for band in range(bands):
                first = part * lats + band * rows
                stack[first : first + rows, :] = data[band, which, part, 0]
        for part in range(2):
            @pl.loop(0, 2)
            def _(i, part=part, target=target):
                at = pl.multiple_of(i * tile, 16)
                value = dot(forward[pl.ds(part * lats + at, tile), :], stack[...])
                target[pl.ds(at, tile), part * half : (part + 1) * half] = value.astype(BF16)

    @pl.loop(0, 2)
    def _(i):
        at = pl.ds(pl.multiple_of(i * tile, 16), tile)
        gelu, slope = gelu_pair(dot(z[at, :], inner[...]))
        hidden[at, :] = gelu.astype(BF16)
        u_adj[at, :] = (dot(back[at, :], outer_t[...]) * slope).astype(BF16)
        z_adj = dot(u_adj[at, :], inner_t[...]).astype(BF16)
        for part in range(2):
            where = pl.ds(pl.multiple_of(part * lats + i * tile, 16), tile)
            stack[where, :] = z_adj[:, part * half : (part + 1) * half]

    outer_total[...] += dot(hidden[...], back[...], 0, 0)
    inner_total[...] += dot(z[...], u_adj[...], 0, 0)
    for part in range(2):
        for band in range(bands):
            first = part * lats + band * rows
            value = dot(backward[first : first + rows, :], stack[...])
            adjoint[band, part, 0] = value.astype(BF16)

    @pl.when(pl.program_id(0) == pl.num_programs(0) - 1)
    def _():
        for which, total in enumerate((inner_total, outer_total)):
            for b in range(half // BLOCK_W):
                low = slice(b * BLOCK_W, (b + 1) * BLOCK_W)
                high = slice(half + b * BLOCK_W, half + (b + 1) * BLOCK_W)
                gradients[which, b, 0] = total[low, low] + total[high, high]
                gradients[which, b, 1] = total[low, high] - total[high, low]


def spectral_filter(first, modes, spectra, forward, backward, inner, inner_t, outer_t, *ties):
    bands, _, _, _, rows, half = spectra.shape
    lats = bands * rows
    wide = 2 * half
    data = pl.BlockSpec((bands, 2, 2, 1, rows, half), lambda i: (0, 0, 0, first + i, 0, 0))

    def whole(*shape):
        return pl.BlockSpec(shape, lambda i: (0,) * len(shape), pipeline_mode=pl.Buffered(1))

    square = whole(2 * lats, 2 * lats)
    weight = whole(wide, wide)
    gradients = (2, half // BLOCK_W, 2, BLOCK_W, BLOCK_W)
    return pl.pallas_call(
        filter_body,
        grid=(modes,),
        in_specs=[data, square, square, weight, weight, weight]
        + [pl.BlockSpec(memory_space=pl.ANY)] * len(ties),
        out_specs=[
            pl.BlockSpec((bands, 2, 1, rows, half), lambda i: (0, 0, i, 0, 0)),
            whole(*gradients),
        ],
        out_shape=[
            jax.ShapeDtypeStruct((bands, 2, modes, rows, half), BF16),
            jax.ShapeDtypeStruct(gradients, F32),
        ],
        scratch_shapes=[
            pltpu.VMEM((2 * lats, half), BF16),
            pltpu.VMEM((lats, wide), BF16),
            pltpu.VMEM((lats, wide), BF16),
            pltpu.VMEM((lats, wide), BF16),
            pltpu.VMEM((lats, wide), BF16),
            pltpu.VMEM((wide, wide), F32),
            pltpu.VMEM((wide, wide), F32),
        ],
        compiler_params=params(),
        cost_estimate=pl.CostEstimate(
            flops=modes * 2 * (3 * 4 * lats * lats * half + 5 * lats * wide * wide),
            bytes_accessed=6 * modes * 2 * lats * half,
            transcendentals=modes * 2 * lats * half * 2,
        ),
        name="spectral_filter",
    )(spectra, forward, backward, inner, inner_t, outer_t, *ties)


def relay_body(t, has_own, has_recv, has_prev, ties, scal, *refs):
    refs = list(refs)
    own = refs.pop(0) if has_own else None
    recv = (refs.pop(0), refs.pop(0)) if has_recv else None
    refs = refs[2 * has_prev + ties :]
    sends, kept = refs[0:2], refs[2:4]
    for way in range(2):
        def put(value, way=way):
            sends[way][...] = value[...]
            kept[way][0] = value[...]

        if own is None:
            put(recv[way])
        elif recv is None:
            put(own)
        else:
            pl.when(scal[t, 2 + way] != 0)(functools.partial(put, own))
            pl.when(scal[t, 2 + way] == 0)(functools.partial(put, recv[way]))


def relay(t, scal, own, own_at, recv, prev, count, shape, ties=()):
    coefs, rows, half = shape
    piece = pl.BlockSpec(shape, lambda i, s: (0, 0, 0))
    in_specs, operands = [], []
    if own is not None:
        in_specs.append(pl.BlockSpec(shape, lambda i, s: (own_at, 0, 0)))
        operands.append(own)
    if recv is not None:
        in_specs += [piece, piece]
        operands += list(recv)
    aliases = {}
    if prev is not None:
        for i, array in enumerate(prev):
            aliases[1 + len(operands)] = 2 + i
            in_specs.append(pl.BlockSpec(memory_space=pl.ANY))
            operands.append(array)
    for array in ties:
        in_specs.append(pl.BlockSpec(memory_space=pl.ANY))
        operands.append(array)

    def kept(way):
        return pl.BlockSpec((1,) + shape, lambda i, s: (s[t, way], 0, 0, 0))

    return pl.pallas_call(
        functools.partial(
            relay_body, t, own is not None, recv is not None, prev is not None, len(ties)
        ),
        grid_spec=pltpu.PrefetchScalarGridSpec(
            num_scalar_prefetch=1,
            grid=(1,),
            in_specs=in_specs,
            out_specs=[piece, piece, kept(0), kept(1)],
        ),
        out_shape=[jax.ShapeDtypeStruct(shape, BF16)] * 2
        + [jax.ShapeDtypeStruct((count + 1,) + shape, BF16)] * 2,
        input_output_aliases=aliases,
        compiler_params=params(),
        cost_estimate=pl.CostEstimate(
            flops=0, bytes_accessed=8 * coefs * rows * half, transcendentals=0
        ),
        name="relay",
    )(scal, *operands)


def grid_body(core, *refs):
    pieces, panels, (own_out, other_out, *totals) = refs[:2], refs[2], refs[-4:]
    count, chunk, row_block, half = pieces[0].shape
    coefs = count * chunk
    tiles = half // LANES
    for total, piece in zip(totals, pieces):
        for j in range(tiles):
            value = piece[:, :, :, pl.ds(j * LANES, LANES)].astype(F32)
            total[j] = value.reshape(coefs * row_block, LANES)
    for h in range(row_block):
        rows = [
            jnp.concatenate(
                [total[j, pl.ds(h, coefs, stride=row_block), :] for j in range(tiles)], axis=1
            ).astype(BF16)
            for total in totals
        ]
        value = jnp.concatenate(rows, axis=0)
        own_out[h] = dot(panels[0], value).astype(BF16)
        other_out[h] = dot(panels[1], value).astype(BF16)


def to_grid(core, kept, panels, first, blocks, row_block, rows, width, whole, ties=()):
    count, chunk, _, half = kept[0].shape
    count -= 1
    cols = panels.shape[1]
    in_specs = [
        pl.BlockSpec((count, chunk, row_block, half), lambda i, s: (0, 0, first + i, 0))
    ] * 2 + [pl.BlockSpec(panels.shape, lambda i, s: (0, 0, 0))]
    operands = list(kept) + [panels]
    aliases = {}
    if whole is not None:
        aliases[1 + len(operands)] = 0
        ties = (whole,) + tuple(ties)
    for array in ties:
        in_specs.append(pl.BlockSpec(memory_space=pl.ANY))
        operands.append(array)
    total = pltpu.VMEM((half // LANES, count * chunk * row_block, LANES), F32)
    return pl.pallas_call(
        grid_body,
        grid_spec=pltpu.PrefetchScalarGridSpec(
            num_scalar_prefetch=1,
            grid=(blocks,),
            in_specs=in_specs,
            out_specs=[
                pl.BlockSpec((row_block, cols, half), lambda i, s: (first + i, 0, s[0])),
                pl.BlockSpec((row_block, cols, half), lambda i, s: (i, 0, 0)),
            ],
            scratch_shapes=[total] * 2,
        ),
        out_shape=[
            jax.ShapeDtypeStruct((rows, cols, width), BF16),
            jax.ShapeDtypeStruct((blocks * row_block, cols, half), BF16),
        ],
        input_output_aliases=aliases,
        compiler_params=params(),
        cost_estimate=pl.CostEstimate(
            flops=8 * blocks * row_block * count * chunk * cols * half,
            bytes_accessed=4 * (count * chunk + cols) * blocks * row_block * half,
            transcendentals=0,
        ),
        name="longitude_grid",
    )(core, *operands)


def place_body(core, piece, whole, out):
    out[...] = piece[...]


def place(core, piece, whole, first, row_block):
    rows, cols, half = piece.shape
    return pl.pallas_call(
        place_body,
        grid_spec=pltpu.PrefetchScalarGridSpec(
            num_scalar_prefetch=1,
            grid=(rows // row_block,),
            in_specs=[
                pl.BlockSpec((row_block, cols, half), lambda i, s: (i, 0, 0)),
                pl.BlockSpec(memory_space=pl.ANY),
            ],
            out_specs=pl.BlockSpec((row_block, cols, half), lambda i, s: (first + i, 0, 1 - s[0])),
        ),
        out_shape=jax.ShapeDtypeStruct(whole.shape, BF16),
        input_output_aliases={2: 0},
        compiler_params=params(),
        name="place",
    )(core, piece, whole)


def pick_body(core, array, *refs):
    refs[-1][...] = array[...]


def pick(core, array, rows, row_block, *ties):
    _, cols, width = array.shape
    half = width // 2
    anywhere = pl.BlockSpec(memory_space=pl.ANY)
    return pl.pallas_call(
        pick_body,
        grid_spec=pltpu.PrefetchScalarGridSpec(
            num_scalar_prefetch=1,
            grid=(rows // row_block,),
            in_specs=[pl.BlockSpec((row_block, cols, half), lambda i, s: (i, 0, 1 - s[0]))]
            + [anywhere] * len(ties),
            out_specs=pl.BlockSpec((row_block, cols, half), lambda i, s: (i, 0, 0)),
        ),
        out_shape=jax.ShapeDtypeStruct((rows, cols, half), BF16),
        compiler_params=params(),
        cost_estimate=pl.CostEstimate(
            flops=0, bytes_accessed=2 * rows * cols * width, transcendentals=0
        ),
        name="pick",
    )(core, array, *ties)


def block_diagonal(blocks):
    count, size, _ = blocks.shape
    eye = jnp.eye(count, dtype=blocks.dtype)
    wide = blocks[:, :, None, :] * eye[:, None, :, None]
    return wide.reshape(count * size, count * size)


def complex_weight(weight):
    real = block_diagonal(weight[:, 0])
    imag = block_diagonal(weight[:, 1])
    return jnp.concatenate(
        [
            jnp.concatenate([real, imag], axis=1),
            jnp.concatenate([-imag, real], axis=1),
        ],
        axis=0,
    )


def local(fields, cotangent, inner_weight, outer_weight):
    lat_count = lax.axis_size("lat")
    lon_count = lax.axis_size("lon")
    rows, cols, width = fields.shape
    chips = lon_count // 2
    half = width // 2
    lon = lax.axis_index("lon")
    chip = lon // 2
    core = lon % 2
    row_block = 16 if rows % 16 == 0 else 8
    blocks = rows // row_block
    per_end = MODES // 2
    per_group = per_end // lat_count
    per_part = per_group // PARTS
    coefs = lat_count * 2 * per_part
    swap = [(i, i ^ 1) for i in range(lon_count)]
    upward = [(i, i + 2) for i in range(lon_count - 2)]
    downward = [(i + 2, i) for i in range(lon_count - 2)]

    core_now = core.reshape(1).astype(jnp.int32)
    early = []
    for array in (fields, cotangent):
        early.append(pick(core_now, array, FIRST * row_block, row_block, *early))
    fields_sent = pick(core_now, fields, rows, row_block, early[1])
    fields_first, cot_first = [lax.ppermute(array, "lon", swap) for array in early]
    fields_other = lax.ppermute(fields_sent, "lon", swap)

    q = jnp.arange(coefs, dtype=jnp.int32)
    part_of = q // per_part % 2
    ids = q // (2 * per_part) * per_group + q % per_part
    ends = jnp.arange(2, dtype=jnp.int32)[:, None, None] * per_end
    pieces = jnp.arange(PARTS, dtype=jnp.int32)[None, :, None] * per_part
    mode_ids = (ends + pieces + ids).reshape(-1)
    imag_row = jnp.tile(part_of, 2 * PARTS) == 1
    places = jnp.concatenate(
        [lon * cols + jnp.arange(cols, dtype=jnp.int32),
         (lon ^ 1) * cols + jnp.arange(cols, dtype=jnp.int32)]
    )
    cos_rows, sin_rows = trig_rows(mode_ids, places, LONS)
    base = jnp.where(imag_row[:, None], -sin_rows, cos_rows)
    weights = jnp.where(mode_ids == 0, 1.0, 2.0).astype(BF16)
    both = jnp.stack([base, base * weights[:, None]], axis=0)
    tables = both.reshape(2, 2, PARTS, coefs, 2, cols).transpose(2, 1, 0, 4, 3, 5)
    some = per_part // 2
    calls = [(s, 0, per_part) for s in range(PARTS - 1)]
    calls += [(PARTS - 1, 0, some), (PARTS - 1, some, per_part - some)]
    by_mode = base.reshape(2, PARTS, 2 * lat_count, per_part, 2, cols)
    panels = jnp.concatenate(
        [by_mode[:, s, :, f : f + n].reshape(2, -1, 2, cols) for s, f, n in calls], axis=1
    )
    panels = panels.transpose(2, 3, 0, 1).reshape(2, cols, 2 * PARTS * coefs)

    lat_ids = jnp.arange(LATS, dtype=jnp.int32)
    lat_cos, lat_sin = trig_rows(lat_ids, lat_ids, LATS)
    forward = jnp.concatenate(
        [jnp.concatenate([lat_cos, lat_sin], axis=1),
         jnp.concatenate([-lat_sin, lat_cos], axis=1)], axis=0
    )
    backward = jnp.concatenate(
        [jnp.concatenate([lat_cos, -lat_sin], axis=1),
         jnp.concatenate([lat_sin, lat_cos], axis=1)], axis=0
    )
    own_blocks = half // BLOCK_W
    inner = complex_weight(
        lax.dynamic_slice_in_dim(inner_weight, core * own_blocks, own_blocks, axis=0)
    )
    outer = complex_weight(
        lax.dynamic_slice_in_dim(outer_weight, core * own_blocks, own_blocks, axis=0)
    )
    inner_t, outer_t = inner.T, outer.T

    order = [(s, r) for s in range(PARTS) for r in range(blocks)]
    count = len(order)
    slots = count + DELAY * (chips - 1)
    slot_ids = jnp.arange(slots, dtype=jnp.int32)

    def schedule(late):
        v = jnp.clip(slot_ids - DELAY * late, 0, count - 1)
        return [v % blocks, v // blocks]

    def has_chunk(late):
        v = slot_ids - DELAY * late
        return ((v >= 0) & (v < count)).astype(jnp.int32)

    flat = jnp.zeros_like(slot_ids)
    hop_plan = jnp.stack(
        schedule(chip)
        + schedule(chips - 1 - chip)
        + [flat + core, flat + chip, has_chunk(chip), has_chunk(chips - 1 - chip)],
        axis=1,
    )
    def across(array):
        return lax.all_to_all(array, "lat", split_axis=0, concat_axis=0, tiled=True)

    last = [fields_sent]
    sent, gathered, every_row, spread, terms = {}, {}, {}, [], []
    others = {"cot": None}

    def hop_slot(t):
        v = t - DELAY * (chips - 1)
        if t < FIRST:
            arrays = (fields, cotangent, fields_first, cot_first)
        else:
            arrays = (fields, cotangent, fields_other, others["cot"])
        recv = sent.pop(t - DELAY, None)
        key, final_at, prev = None, None, None
        if v >= 0:
            key, final_at = order[v]
            prev = gathered.get(key)
        result = hop(
            t, lat_count, hop_plan, arrays, tables, recv, prev, final_at, row_block, rows, last
        )
        last[:] = [result[0]]
        if v >= 0:
            gathered[key] = result[2]
            if final_at == blocks - 1:
                every_row[key] = across(result[2])
        if t < count + DELAY * (chips - 2):
            sent[t] = (
                lax.ppermute(result[0], "lon", upward),
                lax.ppermute(result[1], "lon", downward),
            )
        if t == 0:
            cot_sent = pick(core_now, cotangent, rows, row_block, *last)
            last[:] = [cot_sent]
            others["cot"] = lax.ppermute(cot_sent, "lon", swap)

    def filter_piece(n):
        s, first, some = calls[n]
        spectra = every_row[s].reshape(lat_count, 2, 2, per_part, rows, half)
        adjoint, part = spectral_filter(
            first, some, spectra, forward, backward, inner, inner_t, outer_t, *last
        )
        last[:] = [adjoint]
        terms.append(part)
        array = across(adjoint.reshape(-1, rows, half))
        spread.extend((array, i) for i in range(array.shape[0] // CHUNK))

    def add_up():
        at_end = (chip == 0) | (chip == chips - 1)
        now = jnp.where(at_end, sum(terms), 0.0).reshape(lat_count, -1, LANES)
        return jnp.sum(across(now), axis=0)

    relay_count = PARTS * coefs // CHUNK
    relay_slots = relay_count + DELAY * (chips - 1)
    relay_ids = jnp.arange(relay_slots, dtype=jnp.int32)

    def place_of(late):
        v = relay_ids - DELAY * late
        return jnp.where((v >= 0) & (v < relay_count), v, relay_count)

    flat = jnp.zeros_like(relay_ids)
    relay_plan = jnp.stack(
        [place_of(chip), place_of(chips - 1 - chip),
         flat + (chip == 0), flat + (chip == chips - 1)], axis=1
    ).astype(jnp.int32)
    passed = {}
    kept = []

    def relay_slot(t, *ties):
        own, own_at = (None, None)
        if t < relay_count:
            own, own_at = spread[t]
        up, down, *kept[:] = relay(
            t, relay_plan, own, own_at, passed.pop(t - DELAY, None), tuple(kept) or None,
            relay_count, (CHUNK, rows, half), last + list(ties),
        )
        last[:] = [up]
        if t < relay_count + DELAY * (chips - 2):
            passed[t] = (lax.ppermute(up, "lon", upward), lax.ppermute(down, "lon", downward))

    for t in range(slots):
        if t in (slots - 16, slots - 9, slots - 2):
            filter_piece(len(terms))
        hop_slot(t)
        if t >= slots - 6:
            relay_slot(t - slots + 6)
    for t in range(6, relay_slots):
        if t in (10, 11):
            filter_piece(len(terms))
        ties = []
        if t == 13:
            share = add_up()
            ties.append(share)
            by_core = lax.all_gather(share, "lon").reshape(chips, 2, -1, LANES)
            by_core = jnp.sum(by_core, axis=0)
            sums = lax.all_gather(by_core, "lat", axis=1, tiled=True)
        if t == relay_slots - 1:
            ties.append(by_core)
        relay_slot(t, *ties)

    whole = None
    swapped = []
    for first, some in ((0, blocks - blocks // 2), (blocks - blocks // 2, blocks // 2)):
        whole, for_other = to_grid(
            core_now, kept, panels, first, some, row_block, rows, width, whole,
            (sums,) if first else (),
        )
        swapped.append((first, lax.ppermute(for_other, "lon", swap)))
    for first, piece in swapped:
        whole = place(core_now, piece, whole, first, row_block)
    sums = (sums * (1.0 / math.sqrt(LATS * MODES))).reshape(2, 2, own_blocks, 2, BLOCK_W, BLOCK_W)
    sums = jnp.swapaxes(sums, 0, 1).reshape(2, BLOCKS, 2, BLOCK_W, BLOCK_W)
    return (whole, sums[0], sums[1])


def solution(mesh):
    return jax.shard_map(
        local,
        mesh=mesh,
        in_specs=(P("lat", "lon", None), P("lat", "lon", None), P(), P()),
        out_specs=(P("lat", "lon", None), P(), P()),
        check_vma=False,
    )
```

```python
import functools
import math

import jax
import jax.numpy as jnp
from jax import lax
from jax.experimental import pallas as pl
from jax.experimental.pallas import tpu as pltpu
from jax.sharding import PartitionSpec as P

LATS = 448
LONS = 896
MODES = 128
BLOCKS = 8
BLOCK_W = 96
PARTS = 4
CHUNK = 8
FIRST = 3
DELAY = 2
LANES = 128
VMEM = 62 * 1024 * 1024
F32 = jnp.float32
BF16 = jnp.bfloat16


def trig_rows(row_ids, col_ids, period):
    phase = (row_ids[:, None] * col_ids[None, :] % period).astype(F32) * (2.0 * math.pi / period)
    factor = 1.0 / math.sqrt(period)
    return (
        (jnp.cos(phase) * factor).astype(BF16),
        (jnp.sin(phase) * factor).astype(BF16),
    )


def gelu_pair(value):
    cdf = 0.5 * (1.0 + lax.erf(value * 0.7071067811865476))
    density = jnp.exp(-0.5 * value * value) * 0.3989422804014327
    return (value * cdf, cdf + value * density)


def dot(left, right, left_dim=1, right_dim=0):
    return lax.dot_general(
        left, right, (((left_dim,), (right_dim,)), ((), ())), preferred_element_type=F32
    )


def params():
    return pltpu.CompilerParams(vmem_limit_bytes=VMEM)


def hop_body(t, bands, row_block, has_recv, has_prev, has_final, ties, scal, *refs):
    refs = list(refs)
    fields, cot, fields_other, cot_other, tables = refs[:5]
    at = 5
    recv = refs[at : at + 2] if has_recv else None
    at += 2 * has_recv + has_prev + ties
    outs = refs[at : at + 2]
    at += 2
    final = None
    if has_final is not None:
        final = refs[at]
        at += 1
    x, table, recv_now, total, out, x_sem, table_sem, recv_sem, out_sem, final_sem = refs[at:]
    half = x.shape[-1]
    coefs = out.shape[1]
    share = coefs // (2 * bands)
    tiles = half // LANES
    mine = pl.ds(pl.multiple_of(scal[t, 4] * half, LANES), half)

    def row_copy(way, which, who):
        rows = pl.ds(scal[t, 2 * way] * row_block, row_block)
        array = ((fields, fields_other), (cot, cot_other))[which][who]
        source = array.at[rows] if who else array.at[rows, :, mine]
        return pltpu.make_async_copy(source, x.at[way, which, who], x_sem.at[way, which, who])

    def table_copy(way):
        source = tables.at[scal[t, 2 * way + 1], 1 - way]
        return pltpu.make_async_copy(source, table.at[way], table_sem.at[way])

    def recv_copy(way):
        return pltpu.make_async_copy(recv[way], recv_now.at[way], recv_sem.at[way])

    def out_copy(way):
        return pltpu.make_async_copy(out.at[way], outs[way], out_sem.at[way])

    def final_copy(way):
        target = final.at[:, pl.ds(has_final * row_block, row_block), :]
        return pltpu.make_async_copy(out.at[way], target, final_sem)

    def fetch(way):
        table_copy(way).start()
        for which in range(2):
            for who in range(2):
                row_copy(way, which, who).start()
        if has_recv:
            recv_copy(way).start()

    def work(way):
        table_copy(way).wait()
        for which in range(2):
            for who in range(2):
                row_copy(way, which, who).wait()
            for h in range(row_block):
                value = dot(table[way, which, 0], x[way, which, 0, h])
                value = value + dot(table[way, which, 1], x[way, which, 1, h])
                for band in range(bands):
                    first = (2 * band + which) * share * row_block + h
                    for j in range(tiles):
                        total[j, pl.ds(first, share, stride=row_block), :] = value[
                            band * share : (band + 1) * share, j * LANES : (j + 1) * LANES
                        ]
        if has_recv:
            recv_copy(way).wait()
        for j in range(tiles):
            lanes = pl.ds(j * LANES, LANES)
            value = total[j].reshape(coefs, row_block, LANES)
            if has_recv:
                value = value + recv_now[way, :, :, lanes].astype(F32)
            out[way, :, :, lanes] = value.astype(BF16)
        out_copy(way).start()

    for step in (fetch, work):
        for way in range(2):
            pl.when(scal[t, 6 + way] != 0)(functools.partial(step, way))
    if has_final is not None:
        pl.when(scal[t, 5] == 0)(lambda: final_copy(1).start())
        pl.when(scal[t, 5] != 0)(lambda: final_copy(0).start())
    for way in range(2):
        pl.when(scal[t, 6 + way] != 0)(lambda way=way: out_copy(way).wait())
    if has_final is not None:
        final_copy(0).wait()


def hop(t, bands, scal, arrays, tables, recv, prev, final_at, row_block, rows, ties=()):
    fields, _, fields_other, _ = arrays
    cols = fields.shape[1]
    half = fields_other.shape[2]
    coefs = 2 * tables.shape[4]
    operands = list(arrays) + [tables]
    if recv is not None:
        operands += list(recv)
    aliases = {}
    if prev is not None:
        aliases[1 + len(operands)] = 2
        operands.append(prev)
    operands += list(ties)
    out_shape = [jax.ShapeDtypeStruct((coefs, row_block, half), BF16)] * 2
    if final_at is not None:
        out_shape.append(jax.ShapeDtypeStruct((coefs, rows, half), BF16))
    anywhere = pl.BlockSpec(memory_space=pl.ANY)
    piece = pltpu.VMEM((2, coefs, row_block, half), BF16)
    return pl.pallas_call(
        functools.partial(
            hop_body, t, bands, row_block, recv is not None, prev is not None, final_at, len(ties)
        ),
        grid_spec=pltpu.PrefetchScalarGridSpec(
            num_scalar_prefetch=1,
            grid=(),
            in_specs=[anywhere] * len(operands),
            out_specs=[anywhere] * len(out_shape),
            scratch_shapes=[
                pltpu.VMEM((2, 2, 2, row_block, cols, half), BF16),
                pltpu.VMEM((2,) + tables.shape[2:], BF16),
                piece,
                pltpu.VMEM((half // LANES, coefs * row_block, LANES), F32),
                piece,
                pltpu.SemaphoreType.DMA((2, 2, 2)),
                pltpu.SemaphoreType.DMA((2,)),
                pltpu.SemaphoreType.DMA((2,)),
                pltpu.SemaphoreType.DMA((2,)),
                pltpu.SemaphoreType.DMA,
            ],
        ),
        out_shape=out_shape,
        input_output_aliases=aliases,
        compiler_params=params(),
        cost_estimate=pl.CostEstimate(
            flops=8 * row_block * coefs * cols * half,
            bytes_accessed=24 * row_block * cols * half,
            transcendentals=0,
        ),
        name="longitude_hop",
    )(scal, *operands)


def filter_body(
    data, forward, backward, inner, inner_t, outer_t, *refs,
):
    (adjoint, gradients, stack, z, back, hidden, u_adj, inner_total, outer_total) = refs[-9:]
    bands, _, _, _, rows, half = data.shape
    lats = bands * rows
    tile = lats // 2

    @pl.when(pl.program_id(0) == 0)
    def _():
        inner_total[...] = jnp.zeros_like(inner_total)
        outer_total[...] = jnp.zeros_like(outer_total)

    for which, target in enumerate((z, back)):
        for part in range(2):
            for band in range(bands):
                first = part * lats + band * rows
                stack[first : first + rows, :] = data[band, which, part, 0]
        for part in range(2):
            @pl.loop(0, 2)
            def _(i, part=part, target=target):
                at = pl.multiple_of(i * tile, 16)
                value = dot(forward[pl.ds(part * lats + at, tile), :], stack[...])
                target[pl.ds(at, tile), part * half : (part + 1) * half] = value.astype(BF16)

    @pl.loop(0, 2)
    def _(i):
        at = pl.ds(pl.multiple_of(i * tile, 16), tile)
        gelu, slope = gelu_pair(dot(z[at, :], inner[...]))
        hidden[at, :] = gelu.astype(BF16)
        u_adj[at, :] = (dot(back[at, :], outer_t[...]) * slope).astype(BF16)
        z_adj = dot(u_adj[at, :], inner_t[...]).astype(BF16)
        for part in range(2):
            where = pl.ds(pl.multiple_of(part * lats + i * tile, 16), tile)
            stack[where, :] = z_adj[:, part * half : (part + 1) * half]

    outer_total[...] += dot(hidden[...], back[...], 0, 0)
    inner_total[...] += dot(z[...], u_adj[...], 0, 0)
    for part in range(2):
        for band in range(bands):
            first = part * lats + band * rows
            value = dot(backward[first : first + rows, :], stack[...])
            adjoint[band, part, 0] = value.astype(BF16)

    @pl.when(pl.program_id(0) == pl.num_programs(0) - 1)
    def _():
        for which, total in enumerate((inner_total, outer_total)):
            for b in range(half // BLOCK_W):
                low = slice(b * BLOCK_W, (b + 1) * BLOCK_W)
                high = slice(half + b * BLOCK_W, half + (b + 1) * BLOCK_W)
                gradients[which, b, 0] = total[low, low] + total[high, high]
                gradients[which, b, 1] = total[low, high] - total[high, low]


def spectral_filter(first, modes, spectra, forward, backward, inner, inner_t, outer_t, *ties):
    bands, _, _, _, rows, half = spectra.shape
    lats = bands * rows
    wide = 2 * half
    data = pl.BlockSpec((bands, 2, 2, 1, rows, half), lambda i: (0, 0, 0, first + i, 0, 0))

    def whole(*shape):
        return pl.BlockSpec(shape, lambda i: (0,) * len(shape), pipeline_mode=pl.Buffered(1))

    square = whole(2 * lats, 2 * lats)
    weight = whole(wide, wide)
    gradients = (2, half // BLOCK_W, 2, BLOCK_W, BLOCK_W)
    return pl.pallas_call(
        filter_body,
        grid=(modes,),
        in_specs=[data, square, square, weight, weight, weight]
        + [pl.BlockSpec(memory_space=pl.ANY)] * len(ties),
        out_specs=[
            pl.BlockSpec((bands, 2, 1, rows, half), lambda i: (0, 0, i, 0, 0)),
            whole(*gradients),
        ],
        out_shape=[
            jax.ShapeDtypeStruct((bands, 2, modes, rows, half), BF16),
            jax.ShapeDtypeStruct(gradients, F32),
        ],
        scratch_shapes=[
            pltpu.VMEM((2 * lats, half), BF16),
            pltpu.VMEM((lats, wide), BF16),
            pltpu.VMEM((lats, wide), BF16),
            pltpu.VMEM((lats, wide), BF16),
            pltpu.VMEM((lats, wide), BF16),
            pltpu.VMEM((wide, wide), F32),
            pltpu.VMEM((wide, wide), F32),
        ],
        compiler_params=params(),
        cost_estimate=pl.CostEstimate(
            flops=modes * 2 * (3 * 4 * lats * lats * half + 5 * lats * wide * wide),
            bytes_accessed=6 * modes * 2 * lats * half,
            transcendentals=modes * 2 * lats * half * 2,
        ),
        name="spectral_filter",
    )(spectra, forward, backward, inner, inner_t, outer_t, *ties)


def relay_body(t, has_own, has_recv, has_prev, ties, scal, *refs):
    refs = list(refs)
    own = refs.pop(0) if has_own else None
    recv = (refs.pop(0), refs.pop(0)) if has_recv else None
    refs = refs[2 * has_prev + ties :]
    sends, kept = refs[0:2], refs[2:4]
    for way in range(2):
        def put(value, way=way):
            sends[way][...] = value[...]
            kept[way][0] = value[...]

        if own is None:
            put(recv[way])
        elif recv is None:
            put(own)
        else:
            pl.when(scal[t, 2 + way] != 0)(functools.partial(put, own))
            pl.when(scal[t, 2 + way] == 0)(functools.partial(put, recv[way]))


def relay(t, scal, own, own_at, recv, prev, count, shape, ties=()):
    coefs, rows, half = shape
    piece = pl.BlockSpec(shape, lambda i, s: (0, 0, 0))
    in_specs, operands = [], []
    if own is not None:
        in_specs.append(pl.BlockSpec(shape, lambda i, s: (own_at, 0, 0)))
        operands.append(own)
    if recv is not None:
        in_specs += [piece, piece]
        operands += list(recv)
    aliases = {}
    if prev is not None:
        for i, array in enumerate(prev):
            aliases[1 + len(operands)] = 2 + i
            in_specs.append(pl.BlockSpec(memory_space=pl.ANY))
            operands.append(array)
    for array in ties:
        in_specs.append(pl.BlockSpec(memory_space=pl.ANY))
        operands.append(array)

    def kept(way):
        return pl.BlockSpec((1,) + shape, lambda i, s: (s[t, way], 0, 0, 0))

    return pl.pallas_call(
        functools.partial(
            relay_body, t, own is not None, recv is not None, prev is not None, len(ties)
        ),
        grid_spec=pltpu.PrefetchScalarGridSpec(
            num_scalar_prefetch=1,
            grid=(1,),
            in_specs=in_specs,
            out_specs=[piece, piece, kept(0), kept(1)],
        ),
        out_shape=[jax.ShapeDtypeStruct(shape, BF16)] * 2
        + [jax.ShapeDtypeStruct((count + 1,) + shape, BF16)] * 2,
        input_output_aliases=aliases,
        compiler_params=params(),
        cost_estimate=pl.CostEstimate(
            flops=0, bytes_accessed=8 * coefs * rows * half, transcendentals=0
        ),
        name="relay",
    )(scal, *operands)


def grid_body(core, *refs):
    pieces, panels, (own_out, other_out, *totals) = refs[:2], refs[2], refs[-4:]
    count, chunk, row_block, half = pieces[0].shape
    coefs = count * chunk
    tiles = half // LANES
    for total, piece in zip(totals, pieces):
        for j in range(tiles):
            value = piece[:, :, :, pl.ds(j * LANES, LANES)].astype(F32)
            total[j] = value.reshape(coefs * row_block, LANES)
    for h in range(row_block):
        rows = [
            jnp.concatenate(
                [total[j, pl.ds(h, coefs, stride=row_block), :] for j in range(tiles)], axis=1
            ).astype(BF16)
            for total in totals
        ]
        value = jnp.concatenate(rows, axis=0)
        own_out[h] = dot(panels[0], value).astype(BF16)
        other_out[h] = dot(panels[1], value).astype(BF16)


def to_grid(core, kept, panels, first, blocks, row_block, rows, width, whole, ties=()):
    count, chunk, _, half = kept[0].shape
    count -= 1
    cols = panels.shape[1]
    in_specs = [
        pl.BlockSpec((count, chunk, row_block, half), lambda i, s: (0, 0, first + i, 0))
    ] * 2 + [pl.BlockSpec(panels.shape, lambda i, s: (0, 0, 0))]
    operands = list(kept) + [panels]
    aliases = {}
    if whole is not None:
        aliases[1 + len(operands)] = 0
        ties = (whole,) + tuple(ties)
    for array in ties:
        in_specs.append(pl.BlockSpec(memory_space=pl.ANY))
        operands.append(array)
    total = pltpu.VMEM((half // LANES, count * chunk * row_block, LANES), F32)
    return pl.pallas_call(
        grid_body,
        grid_spec=pltpu.PrefetchScalarGridSpec(
            num_scalar_prefetch=1,
            grid=(blocks,),
            in_specs=in_specs,
            out_specs=[
                pl.BlockSpec((row_block, cols, half), lambda i, s: (first + i, 0, s[0])),
                pl.BlockSpec((row_block, cols, half), lambda i, s: (i, 0, 0)),
            ],
            scratch_shapes=[total] * 2,
        ),
        out_shape=[
            jax.ShapeDtypeStruct((rows, cols, width), BF16),
            jax.ShapeDtypeStruct((blocks * row_block, cols, half), BF16),
        ],
        input_output_aliases=aliases,
        compiler_params=params(),
        cost_estimate=pl.CostEstimate(
            flops=8 * blocks * row_block * count * chunk * cols * half,
            bytes_accessed=4 * (count * chunk + cols) * blocks * row_block * half,
            transcendentals=0,
        ),
        name="longitude_grid",
    )(core, *operands)


def place_body(core, piece, whole, out):
    out[...] = piece[...]


def place(core, piece, whole, first, row_block):
    rows, cols, half = piece.shape
    return pl.pallas_call(
        place_body,
        grid_spec=pltpu.PrefetchScalarGridSpec(
            num_scalar_prefetch=1,
            grid=(rows // row_block,),
            in_specs=[
                pl.BlockSpec((row_block, cols, half), lambda i, s: (i, 0, 0)),
                pl.BlockSpec(memory_space=pl.ANY),
            ],
            out_specs=pl.BlockSpec((row_block, cols, half), lambda i, s: (first + i, 0, 1 - s[0])),
        ),
        out_shape=jax.ShapeDtypeStruct(whole.shape, BF16),
        input_output_aliases={2: 0},
        compiler_params=params(),
        name="place",
    )(core, piece, whole)


def pick_body(core, array, *refs):
    refs[-1][...] = array[...]


def pick(core, array, rows, row_block, *ties):
    _, cols, width = array.shape
    half = width // 2
    anywhere = pl.BlockSpec(memory_space=pl.ANY)
    return pl.pallas_call(
        pick_body,
        grid_spec=pltpu.PrefetchScalarGridSpec(
            num_scalar_prefetch=1,
            grid=(rows // row_block,),
            in_specs=[pl.BlockSpec((row_block, cols, half), lambda i, s: (i, 0, 1 - s[0]))]
            + [anywhere] * len(ties),
            out_specs=pl.BlockSpec((row_block, cols, half), lambda i, s: (i, 0, 0)),
        ),
        out_shape=jax.ShapeDtypeStruct((rows, cols, half), BF16),
        compiler_params=params(),
        cost_estimate=pl.CostEstimate(
            flops=0, bytes_accessed=2 * rows * cols * width, transcendentals=0
        ),
        name="pick",
    )(core, array, *ties)


def block_diagonal(blocks):
    count, size, _ = blocks.shape
    eye = jnp.eye(count, dtype=blocks.dtype)
    wide = blocks[:, :, None, :] * eye[:, None, :, None]
    return wide.reshape(count * size, count * size)


def complex_weight(weight):
    real = block_diagonal(weight[:, 0])
    imag = block_diagonal(weight[:, 1])
    return jnp.concatenate(
        [
            jnp.concatenate([real, imag], axis=1),
            jnp.concatenate([-imag, real], axis=1),
        ],
        axis=0,
    )


def local(fields, cotangent, inner_weight, outer_weight):
    lat_count = lax.axis_size("lat")
    lon_count = lax.axis_size("lon")
    rows, cols, width = fields.shape
    chips = lon_count // 2
    half = width // 2
    lon = lax.axis_index("lon")
    chip = lon // 2
    core = lon % 2
    row_block = 16 if rows % 16 == 0 else 8
    blocks = rows // row_block
    per_end = MODES // 2
    per_group = per_end // lat_count
    per_part = per_group // PARTS
    coefs = lat_count * 2 * per_part
    swap = [(i, i ^ 1) for i in range(lon_count)]
    upward = [(i, i + 2) for i in range(lon_count - 2)]
    downward = [(i + 2, i) for i in range(lon_count - 2)]

    core_now = core.reshape(1).astype(jnp.int32)
    early = []
    for array in (fields, cotangent):
        early.append(pick(core_now, array, FIRST * row_block, row_block, *early))
    fields_sent = pick(core_now, fields, rows, row_block, early[1])
    fields_first, cot_first = [lax.ppermute(array, "lon", swap) for array in early]
    fields_other = lax.ppermute(fields_sent, "lon", swap)

    q = jnp.arange(coefs, dtype=jnp.int32)
    part_of = q // per_part % 2
    ids = q // (2 * per_part) * per_group + q % per_part
    ends = jnp.arange(2, dtype=jnp.int32)[:, None, None] * per_end
    pieces = jnp.arange(PARTS, dtype=jnp.int32)[None, :, None] * per_part
    mode_ids = (ends + pieces + ids).reshape(-1)
    imag_row = jnp.tile(part_of, 2 * PARTS) == 1
    places = jnp.concatenate(
        [lon * cols + jnp.arange(cols, dtype=jnp.int32),
         (lon ^ 1) * cols + jnp.arange(cols, dtype=jnp.int32)]
    )
    cos_rows, sin_rows = trig_rows(mode_ids, places, LONS)
    base = jnp.where(imag_row[:, None], -sin_rows, cos_rows)
    weights = jnp.where(mode_ids == 0, 1.0, 2.0).astype(BF16)
    both = jnp.stack([base, base * weights[:, None]], axis=0)
    tables = both.reshape(2, 2, PARTS, coefs, 2, cols).transpose(2, 1, 0, 4, 3, 5)
    some = per_part // 2
    calls = [(s, 0, per_part) for s in range(PARTS - 1)]
    calls += [(PARTS - 1, 0, some), (PARTS - 1, some, per_part - some)]
    by_mode = base.reshape(2, PARTS, 2 * lat_count, per_part, 2, cols)
    panels = jnp.concatenate(
        [by_mode[:, s, :, f : f + n].reshape(2, -1, 2, cols) for s, f, n in calls], axis=1
    )
    panels = panels.transpose(2, 3, 0, 1).reshape(2, cols, 2 * PARTS * coefs)

    lat_ids = jnp.arange(LATS, dtype=jnp.int32)
    lat_cos, lat_sin = trig_rows(lat_ids, lat_ids, LATS)
    forward = jnp.concatenate(
        [jnp.concatenate([lat_cos, lat_sin], axis=1),
         jnp.concatenate([-lat_sin, lat_cos], axis=1)], axis=0
    )
    backward = jnp.concatenate(
        [jnp.concatenate([lat_cos, -lat_sin], axis=1),
         jnp.concatenate([lat_sin, lat_cos], axis=1)], axis=0
    )
    own_blocks = half // BLOCK_W
    inner = complex_weight(
        lax.dynamic_slice_in_dim(inner_weight, core * own_blocks, own_blocks, axis=0)
    )
    outer = complex_weight(
        lax.dynamic_slice_in_dim(outer_weight, core * own_blocks, own_blocks, axis=0)
    )
    inner_t, outer_t = inner.T, outer.T

    order = [(s, r) for s in range(PARTS) for r in range(blocks)]
    count = len(order)
    slots = count + DELAY * (chips - 1)
    slot_ids = jnp.arange(slots, dtype=jnp.int32)

    def schedule(late):
        v = jnp.clip(slot_ids - DELAY * late, 0, count - 1)
        return [v % blocks, v // blocks]

    def has_chunk(late):
        v = slot_ids - DELAY * late
        return ((v >= 0) & (v < count)).astype(jnp.int32)

    flat = jnp.zeros_like(slot_ids)
    hop_plan = jnp.stack(
        schedule(chip)
        + schedule(chips - 1 - chip)
        + [flat + core, flat + chip, has_chunk(chip), has_chunk(chips - 1 - chip)],
        axis=1,
    )
    def across(array):
        return lax.all_to_all(array, "lat", split_axis=0, concat_axis=0, tiled=True)

    last = [fields_sent]
    sent, gathered, every_row, spread, terms = {}, {}, {}, [], []
    others = {"cot": None}

    def hop_slot(t):
        v = t - DELAY * (chips - 1)
        if t < FIRST:
            arrays = (fields, cotangent, fields_first, cot_first)
        else:
            arrays = (fields, cotangent, fields_other, others["cot"])
        recv = sent.pop(t - DELAY, None)
        key, final_at, prev = None, None, None
        if v >= 0:
            key, final_at = order[v]
            prev = gathered.get(key)
        result = hop(
            t, lat_count, hop_plan, arrays, tables, recv, prev, final_at, row_block, rows, last
        )
        last[:] = [result[0]]
        if v >= 0:
            gathered[key] = result[2]
            if final_at == blocks - 1:
                every_row[key] = across(result[2])
        if t < count + DELAY * (chips - 2):
            sent[t] = (
                lax.ppermute(result[0], "lon", upward),
                lax.ppermute(result[1], "lon", downward),
            )
        if t == 0:
            cot_sent = pick(core_now, cotangent, rows, row_block, *last)
            last[:] = [cot_sent]
            others["cot"] = lax.ppermute(cot_sent, "lon", swap)

    def filter_piece(n):
        s, first, some = calls[n]
        spectra = every_row[s].reshape(lat_count, 2, 2, per_part, rows, half)
        adjoint, part = spectral_filter(
            first, some, spectra, forward, backward, inner, inner_t, outer_t, *last
        )
        last[:] = [adjoint]
        terms.append(part)
        array = across(adjoint.reshape(-1, rows, half))
        spread.extend((array, i) for i in range(array.shape[0] // CHUNK))

    def add_up():
        at_end = (chip == 0) | (chip == chips - 1)
        now = jnp.where(at_end, sum(terms), 0.0).reshape(lat_count, -1, LANES)
        return jnp.sum(across(now), axis=0)

    relay_count = PARTS * coefs // CHUNK
    relay_slots = relay_count + DELAY * (chips - 1)
    relay_ids = jnp.arange(relay_slots, dtype=jnp.int32)

    def place_of(late):
        v = relay_ids - DELAY * late
        return jnp.where((v >= 0) & (v < relay_count), v, relay_count)

    flat = jnp.zeros_like(relay_ids)
    relay_plan = jnp.stack(
        [place_of(chip), place_of(chips - 1 - chip),
         flat + (chip == 0), flat + (chip == chips - 1)], axis=1
    ).astype(jnp.int32)
    passed = {}
    kept = []

    def relay_slot(t, *ties):
        own, own_at = (None, None)
        if t < relay_count:
            own, own_at = spread[t]
        up, down, *kept[:] = relay(
            t, relay_plan, own, own_at, passed.pop(t - DELAY, None), tuple(kept) or None,
            relay_count, (CHUNK, rows, half), last + list(ties),
        )
        last[:] = [up]
        if t < relay_count + DELAY * (chips - 2):
            passed[t] = (lax.ppermute(up, "lon", upward), lax.ppermute(down, "lon", downward))

    for t in range(slots):
        if t in (slots - 16, slots - 9, slots - 4):
            filter_piece(len(terms))
        if t >= slots - 6:
            relay_slot(t - slots + 6)
        hop_slot(t)
    for t in range(6, relay_slots):
        if t == 10:
            filter_piece(len(terms))
            filter_piece(len(terms))
        ties = []
        if t == 13:
            share = add_up()
            ties.append(share)
            by_core = lax.all_gather(share, "lon").reshape(chips, 2, -1, LANES)
            by_core = jnp.sum(by_core, axis=0)
            sums = lax.all_gather(by_core, "lat", axis=1, tiled=True)
        if t == relay_slots - 1:
            ties.append(by_core)
        relay_slot(t, *ties)

    whole = None
    swapped = []
    for first, some in ((0, blocks - blocks // 2), (blocks - blocks // 2, blocks // 2)):
        whole, for_other = to_grid(
            core_now, kept, panels, first, some, row_block, rows, width, whole,
            (sums,) if first else (),
        )
        swapped.append((first, lax.ppermute(for_other, "lon", swap)))
    for first, piece in swapped:
        whole = place(core_now, piece, whole, first, row_block)
    sums = (sums * (1.0 / math.sqrt(LATS * MODES))).reshape(2, 2, own_blocks, 2, BLOCK_W, BLOCK_W)
    sums = jnp.swapaxes(sums, 0, 1).reshape(2, BLOCKS, 2, BLOCK_W, BLOCK_W)
    return (whole, sums[0], sums[1])


def solution(mesh):
    return jax.shard_map(
        local,
        mesh=mesh,
        in_specs=(P("lat", "lon", None), P("lat", "lon", None), P(), P()),
        out_specs=(P("lat", "lon", None), P(), P()),
        check_vma=False,
    )
```
